32 devices in a mesh: grp: 2 (over y), row: 4 (over z), col: 4 (over x, core).
Axes of the slice: x: 2, y: 2, z: 4, core: 2. Of those that a mesh axis runs over, the one named last changes fastest.
Arguments:
- src_raw: bfloat16 [8, 2, 512, 1024], P(('grp', 'row'), None, 'col'), parts along dimension 0, may hold values from -36 to 36
- block_owner: int32 [4, 4], P('grp', 'col'), parts along dimension 0, may hold values from 0 to 3, as said below
- chan_order: int32 [4, 4, 128], P('grp', 'col'), parts along dimension 0, may hold values from 0 to 127, each once within a row
- rec_raw: bfloat16 [4, 16, 1024], P('grp', ('row', 'col')), parts along dimension 0, may hold values from -36 to 36
- fir_taps: bfloat16 [129], replicated, may hold values from -0.5 to 0.5
- stacks: float32 [1024, 1024], P(('grp', 'col'), 'row'), parts along dimension 0, may hold values from -6 to 6
Outputs:
- new_stacks: float32 [1024, 1024], P(('grp', 'col'), 'row'), parts along dimension 0
The draws below stay inside these ranges and needn't reach their ends.
There are 2 independent parts, one for each index of `grp`. The reference program is written for one: setup_inputs(seed, part) draws one part's arguments, and reference() takes and returns one part's arrays. A program takes and returns all parts, laid end to end along the dimension named above; an argument that names none is the same for every part. Nothing has to cross between parts.
Inputs may be any that keep to these rules, and one draw needn't show every extreme that they name: block_owner[w, c] is the row index whose buffer holds column block c's traces in window w; 0 and 3 both occur in every draw.
All inputs are finite; a program needn't handle non-finite values.
Results may differ from the reference program's by a relative error of at most 0.0018.
Values may be sent and summed in bfloat16 or wider, within the bound.
A program may use at most 64 MiB of HBM per device.

```python
import math
import jax
import jax.numpy as jnp
from jax import lax

L = 1024
W = 2
TAPS = 129
LAGS = 64
BLK = 128
S = 512
QROW = 4
OWNERS = 4
R = 16
N_COL = 4


def draw_src_raw(key, part):
    sub_keys = jax.random.split(jax.random.fold_in(key, 11), 3)
    full_shape = (OWNERS, W, S, L)
    chan_scale = jnp.exp(jax.random.uniform(sub_keys[0], (1, 1, S, 1), jnp.float32, jnp.log(0.3), jnp.log(3.0)))
    time_scale = jnp.exp(jax.random.uniform(sub_keys[1], (1, W, 1, L), jnp.float32, jnp.log(0.3), jnp.log(3.0)))
    noise_field = jnp.clip(jax.random.normal(sub_keys[2], full_shape, jnp.float32), -4.0, 4.0)
    return (noise_field * chan_scale * time_scale).astype(jnp.bfloat16)


def draw_rec_raw(key, part):
    sub_keys = jax.random.split(jax.random.fold_in(key, 23), 3)
    full_shape = (W, R, L)
    chan_scale = jnp.exp(jax.random.uniform(sub_keys[0], (1, R, 1), jnp.float32, jnp.log(0.3), jnp.log(3.0)))
    time_scale = jnp.exp(jax.random.uniform(sub_keys[1], (W, 1, L), jnp.float32, jnp.log(0.3), jnp.log(3.0)))
    noise_field = jnp.clip(jax.random.normal(sub_keys[2], full_shape, jnp.float32), -4.0, 4.0)
    return (noise_field * chan_scale * time_scale).astype(jnp.bfloat16)


def draw_block_owner(key, part):
    sub_keys = jax.random.split(jax.random.fold_in(key, 37), 2)
    total = W * N_COL
    owners_flat = jax.random.randint(sub_keys[0], (total,), 0, OWNERS)
    positions = jax.random.permutation(sub_keys[1], total)
    owners_flat = owners_flat.at[positions[0]].set(0)
    owners_flat = owners_flat.at[positions[1]].set(OWNERS - 1)
    return owners_flat.reshape((W, N_COL)).astype(jnp.int32)


def level_of(own_key, extent, shards, least, largest):
    def one(axis_at, blocks):
        heights = jax.random.uniform(jax.random.fold_in(jax.random.fold_in(own_key, 6), axis_at), (blocks,), jnp.float32, least / len(shards), largest / len(shards))
        return jnp.repeat(jnp.exp(heights), extent[axis_at] // blocks).reshape((-1,) + (1,) * (len(extent) - axis_at - 1))

    level = one(*shards[0])
    for cut in shards[1:]:
        level = level * one(*cut)
    return level


def centred(key, dims, spread, most, cuts=(), kind=jnp.bfloat16):
    array = jax.random.normal(key, dims, jnp.float32) * spread
    if len(cuts) > 0:
        array = level_of(key, dims, cuts, -0.22, 0.18) * array
    return jnp.clip(array, min=-most, max=most).astype(kind)


def setup_inputs(seed: int = 0, part: int = 0) -> dict:
    arg_keys = jax.random.split(jax.random.key(seed), 7)
    own_keys = jax.random.split(jax.random.fold_in(arg_keys[6], part), 7)
    src_raw = draw_src_raw(jax.random.fold_in(jax.random.fold_in(arg_keys[6], part), 71), part)
    block_owner = draw_block_owner(jax.random.fold_in(jax.random.fold_in(arg_keys[6], part), 71), part)
    chan_order = jax.vmap(lambda own: jax.random.permutation(own, BLK))(jax.random.split(own_keys[2], W * N_COL)).reshape((W, N_COL, BLK)).astype(jnp.int32)
    rec_raw = draw_rec_raw(jax.random.fold_in(jax.random.fold_in(arg_keys[6], part), 71), part)
    fir_taps = centred(arg_keys[4], (TAPS,), TAPS ** -0.5, 0.5)
    stacks = centred(own_keys[5], (S, R * LAGS), 1.0, 6.0, ((0, 4), (1, 4)), jnp.float32)
    return {"src_raw": src_raw, "block_owner": block_owner, "chan_order": chan_order, "rec_raw": rec_raw, "fir_taps": fir_taps, "stacks": stacks}


def apply_filter(raw, fir_taps):
    half_taps = (TAPS - 1) // 2
    padded = jnp.pad(raw.astype(jnp.float32), [(0, 0)] * (raw.ndim - 1) + [(half_taps, half_taps)])
    tap_values = fir_taps.astype(jnp.float32)
    result = jnp.zeros(raw.shape, jnp.float32)
    for offset in range(TAPS):
        result = result + tap_values[offset] * padded[..., offset:offset + L]
    return result.astype(jnp.bfloat16)

def pair_terms(source_rows, src_energy, rec_rows):
    count = rec_rows.shape[0]
    half_lags = LAGS // 2
    padded = jnp.pad(rec_rows.astype(jnp.float32), ((0, 0), (half_lags, LAGS - half_lags)))
    hankel = jnp.stack([padded[:, offset:offset + L] for offset in range(LAGS)], axis=1)
    hankel = hankel.reshape((count * LAGS, L))
    lagged = jnp.dot(source_rows.astype(jnp.float32), hankel.T, precision=lax.Precision.HIGHEST)
    rec_energy = lax.optimization_barrier(jnp.sum(jnp.square(rec_rows.astype(jnp.float32)), axis=1))
    scale_pair = lax.rsqrt(src_energy[:, None, None] * rec_energy[None, :, None] + 1e-06)
    ratio = lagged.reshape((source_rows.shape[0], count, LAGS)) * scale_pair
    return jnp.tanh(0.5 * math.sqrt(L) * ratio).reshape((source_rows.shape[0], count * LAGS))

def reference(src_raw, block_owner, chan_order, rec_raw, fir_taps, stacks):
    receivers = apply_filter(rec_raw, fir_taps)
    updated = stacks
    for window in range(W):
        blocks = []
        for column in range(S // BLK):
            owner_row = block_owner[window, column].astype(jnp.int32)
            owner_rows = lax.dynamic_index_in_dim(src_raw, owner_row, 0, keepdims=False)
            block_rows = owner_rows[window, column * BLK:(column + 1) * BLK]
            blocks.append(jnp.take(block_rows, chan_order[window, column].astype(jnp.int32), axis=0))
        sources = apply_filter(jnp.concatenate(blocks, axis=0), fir_taps)
        src_energy = lax.optimization_barrier(jnp.sum(jnp.square(sources.astype(jnp.float32)), axis=1))
        rec_groups = receivers[window].reshape((R // QROW, QROW, L))
        terms = lax.map(lambda rec_rows: pair_terms(sources, src_energy, rec_rows), rec_groups)
        updated = updated + jnp.transpose(terms, (1, 0, 2)).reshape((S, R * LAGS))
    return updated
```

```python
import functools
import math

import jax
import jax.numpy as jnp
from jax import lax
from jax.experimental import pallas as pl
from jax.experimental.pallas import tpu as pltpu
from jax.sharding import PartitionSpec as P

MESH = pl.DeviceIdType.MESH
LANES = 128
OUT_TILE = 256
NT = (((1,), (1,)), ((), ()))
TN = (((0,), (0,)), ((), ()))


def steps(count, body):
    if count <= 4:
        for index in range(count):
            body(index)
    else:
        pl.loop(0, count)(body)


def kernel(
    n_row, n_col, half_taps, lags,
    owner_ref, order_ref, taps_ref, rec_ref, src_ref, stacks_ref,
    out_ref,
    padded, sources, rec_padded, rec_block, rec_all, hankel, own_sum, sent, landed,
    rec_send, rec_recv, sum_send, sum_recv,
):
    row, col = lax.axis_index("row"), lax.axis_index("col")
    here = row * n_col + col
    windows, per_device, length = rec_ref.shape
    block = src_ref.shape[2]
    half_lags = lags // 2
    tiles = length // LANES
    out_tiles = length // OUT_TILE
    reach = OUT_TILE + 2 * LANES

    barrier = pltpu.get_barrier_semaphore()

    def greet(step):
        other = lax.rem(here + step + 1, n_row * n_col)
        pl.semaphore_signal(
            barrier, inc=1,
            device_id={"row": other // n_col, "col": lax.rem(other, n_col)},
            device_id_type=MESH,
        )

    steps(n_row * n_col - 1, greet)

    band = pltpu.roll(
        jnp.broadcast_to(taps_ref[...], (OUT_TILE, reach)),
        LANES - half_taps, axis=1, stride=1, stride_axis=0,
    ).astype(jnp.bfloat16)
    flip_row = lax.broadcasted_iota(jnp.int32, (OUT_TILE, OUT_TILE), 0)
    flip_col = lax.broadcasted_iota(jnp.int32, (OUT_TILE, OUT_TILE), 1)
    flip = jnp.where(flip_row + flip_col == OUT_TILE - 1, 1.0, 0.0).astype(jnp.bfloat16)
    band = jnp.dot(flip, band, preferred_element_type=jnp.float32).astype(jnp.bfloat16)

    rec_padded[...] = jnp.zeros_like(rec_padded)
    for window in range(windows):
        for index in range(per_device):
            at = window * per_device + index
            rec_padded[at : at + 1, LANES : LANES + length] = rec_ref[
                window, index : index + 1
            ].astype(jnp.float32)
    for tile in range(out_tiles):
        taken = rec_padded[:, tile * OUT_TILE : tile * OUT_TILE + reach].astype(jnp.bfloat16)
        made = lax.dot_general(taken, band, NT, preferred_element_type=jnp.float32)
        for part in range(OUT_TILE // LANES):
            place = (out_tiles - 1 - tile) * (OUT_TILE // LANES) + part
            for at in range(windows * per_device):
                rec_block[at * tiles + place : at * tiles + place + 1, :] = made[
                    at : at + 1, part * LANES : (part + 1) * LANES
                ]
    rec_all[here] = rec_block[...].astype(jnp.bfloat16)

    pl.semaphore_wait(barrier, n_row * n_col - 1)

    def rec_copy(other, slot):
        return pltpu.make_async_remote_copy(
            src_ref=rec_all.at[slot], dst_ref=rec_all.at[slot],
            send_sem=rec_send.at[other], recv_sem=rec_recv.at[slot],
            device_id={"row": other // n_col, "col": lax.rem(other, n_col)},
            device_id_type=MESH,
        )

    def send_rec(step):
        rec_copy(lax.rem(here + step + 1, n_row * n_col), here).start()

    steps(n_row * n_col - 1, send_rec)

    padded[:, :LANES] = jnp.zeros((windows * block, LANES), jnp.bfloat16)
    padded[:, LANES + length :] = jnp.zeros((windows * block, LANES), jnp.bfloat16)
    for window in range(windows):
        position = lax.broadcasted_iota(jnp.int32, (block, block), 0)
        wanted = jnp.where(
            owner_ref[window, 0] == row, order_ref[window : window + 1, :], -1
        )
        chosen = jnp.where(position == wanted, 1.0, 0.0).astype(jnp.bfloat16)
        padded[window * block : (window + 1) * block, LANES : LANES + length] = lax.dot_general(
            chosen, src_ref[0, window], TN, preferred_element_type=jnp.float32
        ).astype(jnp.bfloat16)
    src_energy = jnp.zeros((windows * block, 1), jnp.float32)
    for tile in range(out_tiles):
        made = lax.dot_general(
            padded[:, tile * OUT_TILE : tile * OUT_TILE + reach], band, NT,
            preferred_element_type=jnp.float32,
        ).astype(jnp.bfloat16)
        place = (out_tiles - 1 - tile) * OUT_TILE
        sources[:, place : place + OUT_TILE] = made
        src_energy += jnp.sum(jnp.square(made.astype(jnp.float32)), axis=1, keepdims=True)

    lag = lax.broadcasted_iota(jnp.int32, (half_lags, LANES), 0)
    lane = lax.broadcasted_iota(jnp.int32, (half_lags, LANES), 1)
    from_tile = lane < LANES - half_lags + lag
    from_tile_late = lane >= lag
    nothing = jnp.zeros((lags, LANES), jnp.float32)

    def terms_for(target):
        total = None
        for window in range(windows):
            energies = []
            for column in range(n_col):
                for index in range(per_device):
                    first = (window * per_device + index) * tiles
                    trace = rec_all[target * n_col + column].astype(jnp.float32)[
                        first : first + tiles, :
                    ]
                    energy = jnp.sum(
                        jnp.sum(jnp.square(trace), axis=0, keepdims=True), axis=1, keepdims=True
                    )
                    energies.append(jnp.broadcast_to(energy, (1, lags)))
                    turned = [
                        pltpu.roll(
                            jnp.broadcast_to(trace[tile : tile + 1, :], (lags, LANES)),
                            LANES - half_lags, axis=1, stride=1, stride_axis=0,
                        )
                        for tile in range(tiles)
                    ]
                    turned = [nothing] + turned + [nothing]
                    base = (column * per_device + index) * lags
                    for tile in range(tiles):
                        columns = slice(tile * LANES, (tile + 1) * LANES)
                        hankel[window, base : base + half_lags, columns] = jnp.where(
                            from_tile, turned[tile + 1][:half_lags], turned[tile + 2][:half_lags]
                        ).astype(jnp.bfloat16)
                        hankel[window, base + half_lags : base + lags, columns] = jnp.where(
                            from_tile_late, turned[tile + 1][half_lags:], turned[tile][half_lags:]
                        ).astype(jnp.bfloat16)
            rec_energy = jnp.concatenate(energies, axis=1)
            rows = slice(window * block, (window + 1) * block)
            lagged = lax.dot_general(
                sources[rows, :], hankel[window], NT, preferred_element_type=jnp.float32
            )
            scale_pair = lax.rsqrt(src_energy[rows] * rec_energy + 1e-06)
            term = jnp.tanh(0.5 * math.sqrt(length) * (lagged * scale_pair))
            total = term if total is None else total + term
        return total

    def wait_rec(target, skip):
        def one(column):
            slot = target * n_col + column
            if not skip:
                rec_copy(slot, slot).wait_recv()
        for column in range(n_col):
            one(column)

    def sum_copy(other, slot):
        return pltpu.make_async_remote_copy(
            src_ref=sent.at[other], dst_ref=landed.at[slot],
            send_sem=sum_send.at[other], recv_sem=sum_recv.at[slot],
            device_id={"row": other}, device_id_type=MESH,
        )

    def send_sum(step):
        shift = n_row // 2 + step
        shift = shift + (shift >= n_row) if isinstance(shift, int) else jnp.where(
            shift >= n_row, shift + 1, shift
        )
        target = lax.rem(row + shift, n_row)
        wait_rec(target, False)
        sent[target] = terms_for(target).astype(jnp.bfloat16)
        sum_copy(target, row).start()

    steps(n_row - 1, send_sum)

    for step in range(n_col - 1):
        slot = row * n_col + lax.rem(col + step + 1, n_col)
        rec_copy(slot, slot).wait_recv()
    own_sum[...] = stacks_ref[...] + terms_for(row)

    def add_sum(step):
        other = lax.rem(row + n_row // 2 + step + (step + n_row // 2 >= n_row), n_row)
        sum_copy(other, other).wait_recv()
        own_sum[...] += landed[other].astype(jnp.float32)

    steps(n_row - 1, add_sum)
    out_ref[...] = own_sum[...]

    def sum_sent(step):
        sum_copy(lax.rem(row + step + 1, n_row), row).wait_send()

    def rec_sent(step):
        rec_copy(lax.rem(here + step + 1, n_row * n_col), here).wait_send()

    steps(n_row - 1, sum_sent)
    steps(n_row * n_col - 1, rec_sent)


def shards(n_row, n_col, src_raw, block_owner, chan_order, rec_raw, fir_taps, stacks):
    windows, per_device, length = rec_raw.shape
    block, columns = stacks.shape
    taps = fir_taps.shape[0]
    reach = OUT_TILE + 2 * LANES
    lags = columns // (n_col * per_device)
    devices = n_row * n_col
    tiles = length // LANES
    rec_rows = windows * per_device * tiles
    taps_row = jnp.pad(fir_taps.astype(jnp.float32), (0, reach - taps)).reshape((1, reach))
    vmem = pl.BlockSpec(memory_space=pltpu.VMEM)
    smem = pl.BlockSpec(memory_space=pltpu.SMEM)
    return pl.pallas_call(
        functools.partial(kernel, n_row, n_col, (taps - 1) // 2, lags),
        out_shape=jax.ShapeDtypeStruct(stacks.shape, stacks.dtype),
        in_specs=[smem, vmem, vmem, vmem, vmem, vmem],
        out_specs=vmem,
        scratch_shapes=[
            pltpu.VMEM((windows * block, length + 2 * LANES), jnp.bfloat16),
            pltpu.VMEM((windows * block, length), jnp.bfloat16),
            pltpu.VMEM((-(-windows * per_device // 16) * 16, length + 2 * LANES), jnp.float32),
            pltpu.VMEM((rec_rows, LANES), jnp.float32),
            pltpu.VMEM((devices, rec_rows, LANES), jnp.bfloat16),
            pltpu.VMEM((windows, columns, length), jnp.bfloat16),
            pltpu.VMEM((block, columns), jnp.float32),
            pltpu.VMEM((n_row, block, columns), jnp.bfloat16),
            pltpu.VMEM((n_row, block, columns), jnp.bfloat16),
            pltpu.SemaphoreType.DMA((devices,)),
            pltpu.SemaphoreType.DMA((devices,)),
            pltpu.SemaphoreType.DMA((n_row,)),
            pltpu.SemaphoreType.DMA((n_row,)),
        ],
        compiler_params=pltpu.CompilerParams(
            collective_id=0, has_side_effects=True, vmem_limit_bytes=32 * 1024 * 1024
        ),
        cost_estimate=pl.CostEstimate(
            flops=2 * windows * block * length * columns * n_row,
            transcendentals=2 * windows * block * columns * n_row,
            bytes_accessed=2 * windows * block * length + 8 * block * columns,
        ),
    )(
        block_owner, chan_order.reshape((windows, block)), taps_row, rec_raw, src_raw, stacks
    )


def solution(mesh):
    in_specs = (
        P(("grp", "row"), None, "col", None),
        P("grp", "col"),
        P("grp", "col", None),
        P("grp", ("row", "col"), None),
        P(),
        P(("grp", "col"), "row"),
    )
    out_specs = P(("grp", "col"), "row")
    body = functools.partial(shards, mesh.shape["row"], mesh.shape["col"])
    return jax.shard_map(body, mesh=mesh, in_specs=in_specs, out_specs=out_specs, check_vma=False)
```

```python
import functools
import math

import jax
import jax.numpy as jnp
from jax import lax
from jax.experimental import pallas as pl
from jax.experimental.pallas import tpu as pltpu
from jax.sharding import PartitionSpec as P

MESH = pl.DeviceIdType.MESH
LANES = 128
OUT_TILE = 256
NT = (((1,), (1,)), ((), ()))
TN = (((0,), (0,)), ((), ()))


def steps(count, body):
    if count <= 4:
        for index in range(count):
            body(index)
    else:
        pl.loop(0, count)(body)


def kernel(
    n_row, n_col, half_taps, lags,
    owner_hbm, order_hbm, taps_hbm, rec_hbm, src_hbm, stacks_hbm,
    out_ref,
    owner_ref, order_ref, taps_ref, rec_ref, src_ref, stacks_ref, taps_row, padded, sources, rec_padded, rec_block, rec_all, hankel, own_sum, sent, landed,
    rec_send, rec_recv, sum_send, sum_recv, load_sem,
):
    row, col = lax.axis_index("row"), lax.axis_index("col")
    here = row * n_col + col
    per_device, windows, length = rec_ref.shape
    block = src_ref.shape[2]
    half_lags = lags // 2
    tiles = length // LANES
    out_tiles = length // OUT_TILE
    reach = OUT_TILE + 2 * LANES

    fetched = [
        pltpu.make_async_copy(source, target, load_sem.at[index])
        for index, (source, target) in enumerate([
            (taps_hbm, taps_ref), (rec_hbm, rec_ref), (src_hbm, src_ref),
            (order_hbm, order_ref), (owner_hbm, owner_ref), (stacks_hbm, stacks_ref),
        ])
    ]
    for copy in fetched:
        copy.start()
    fetch_taps, fetch_rec, fetch_src, fetch_order, fetch_owner, fetch_stacks = fetched

    barrier = pltpu.get_barrier_semaphore()

    def greet(step):
        other = lax.rem(here + step + 1, n_row * n_col)
        pl.semaphore_signal(
            barrier, inc=1,
            device_id={"row": other // n_col, "col": lax.rem(other, n_col)},
            device_id_type=MESH,
        )

    steps(n_row * n_col - 1, greet)

    taps_row[...] = jnp.zeros_like(taps_row)
    fetch_taps.wait()
    taps_row[:, : taps_ref.shape[0]] = taps_ref[...].astype(jnp.float32).reshape((1, -1))
    band = pltpu.roll(
        jnp.broadcast_to(taps_row[...], (OUT_TILE, reach)),
        LANES - half_taps, axis=1, stride=1, stride_axis=0,
    ).astype(jnp.bfloat16)
    flip_row = lax.broadcasted_iota(jnp.int32, (OUT_TILE, OUT_TILE), 0)
    flip_col = lax.broadcasted_iota(jnp.int32, (OUT_TILE, OUT_TILE), 1)
    flip = jnp.where(flip_row + flip_col == OUT_TILE - 1, 1.0, 0.0).astype(jnp.bfloat16)
    band = jnp.dot(flip, band, preferred_element_type=jnp.float32).astype(jnp.bfloat16)

    rec_padded[...] = jnp.zeros_like(rec_padded)
    fetch_rec.wait()
    for window in range(windows):
        for index in range(per_device):
            at = window * per_device + index
            rec_padded[at : at + 1, LANES : LANES + length] = rec_ref[
                index, window : window + 1
            ].astype(jnp.float32)
    for tile in range(out_tiles):
        taken = rec_padded[:, tile * OUT_TILE : tile * OUT_TILE + reach].astype(jnp.bfloat16)
        made = lax.dot_general(taken, band, NT, preferred_element_type=jnp.float32)
        for part in range(OUT_TILE // LANES):
            place = (out_tiles - 1 - tile) * (OUT_TILE // LANES) + part
            for at in range(windows * per_device):
                rec_block[at * tiles + place : at * tiles + place + 1, :] = made[
                    at : at + 1, part * LANES : (part + 1) * LANES
                ]
    rec_all[here] = rec_block[...].astype(jnp.bfloat16)

    pl.semaphore_wait(barrier, n_row * n_col - 1)

    def rec_copy(other, slot):
        return pltpu.make_async_remote_copy(
            src_ref=rec_all.at[slot], dst_ref=rec_all.at[slot],
            send_sem=rec_send.at[other], recv_sem=rec_recv.at[slot],
            device_id={"row": other // n_col, "col": lax.rem(other, n_col)},
            device_id_type=MESH,
        )

    def send_rec(step):
        rec_copy(lax.rem(here + step + 1, n_row * n_col), here).start()

    steps(n_row * n_col - 1, send_rec)

    padded[:, :LANES] = jnp.zeros((windows * block, LANES), jnp.bfloat16)
    padded[:, LANES + length :] = jnp.zeros((windows * block, LANES), jnp.bfloat16)
    fetch_src.wait()
    fetch_order.wait()
    fetch_owner.wait()
    for window in range(windows):
        position = lax.broadcasted_iota(jnp.int32, (block, block), 0)
        wanted = jnp.where(
            jnp.broadcast_to(owner_ref[:, window : window + 1], (1, block)) == row,
            order_ref[window], -1,
        )
        chosen = jnp.where(position == wanted, 1.0, 0.0).astype(jnp.bfloat16)
        padded[window * block : (window + 1) * block, LANES : LANES + length] = lax.dot_general(
            chosen, src_ref[0, window], TN, preferred_element_type=jnp.float32
        ).astype(jnp.bfloat16)
    src_energy = jnp.zeros((windows * block, 1), jnp.float32)
    for tile in range(out_tiles):
        made = lax.dot_general(
            padded[:, tile * OUT_TILE : tile * OUT_TILE + reach], band, NT,
            preferred_element_type=jnp.float32,
        ).astype(jnp.bfloat16)
        place = (out_tiles - 1 - tile) * OUT_TILE
        sources[:, place : place + OUT_TILE] = made
        src_energy += jnp.sum(jnp.square(made.astype(jnp.float32)), axis=1, keepdims=True)

    lag = lax.broadcasted_iota(jnp.int32, (half_lags, LANES), 0)
    lane = lax.broadcasted_iota(jnp.int32, (half_lags, LANES), 1)
    from_tile = lane < LANES - half_lags + lag
    from_tile_late = lane >= lag
    nothing = jnp.zeros((lags, LANES), jnp.float32)

    def terms_for(target):
        total = None
        for window in range(windows):
            energies = []
            for column in range(n_col):
                for index in range(per_device):
                    first = (window * per_device + index) * tiles
                    trace = rec_all[target * n_col + column].astype(jnp.float32)[
                        first : first + tiles, :
                    ]
                    energy = jnp.sum(
                        jnp.sum(jnp.square(trace), axis=0, keepdims=True), axis=1, keepdims=True
                    )
                    energies.append(jnp.broadcast_to(energy, (1, lags)))
                    turned = [
                        pltpu.roll(
                            jnp.broadcast_to(trace[tile : tile + 1, :], (lags, LANES)),
                            LANES - half_lags, axis=1, stride=1, stride_axis=0,
                        )
                        for tile in range(tiles)
                    ]
                    turned = [nothing] + turned + [nothing]
                    base = (column * per_device + index) * lags
                    for tile in range(tiles):
                        columns = slice(tile * LANES, (tile + 1) * LANES)
                        hankel[window, base : base + half_lags, columns] = jnp.where(
                            from_tile, turned[tile + 1][:half_lags], turned[tile + 2][:half_lags]
                        ).astype(jnp.bfloat16)
                        hankel[window, base + half_lags : base + lags, columns] = jnp.where(
                            from_tile_late, turned[tile + 1][half_lags:], turned[tile][half_lags:]
                        ).astype(jnp.bfloat16)
            rec_energy = jnp.concatenate(energies, axis=1)
            rows = slice(window * block, (window + 1) * block)
            lagged = lax.dot_general(
                sources[rows, :], hankel[window], NT, preferred_element_type=jnp.float32
            )
            scale_pair = lax.rsqrt(src_energy[rows] * rec_energy + 1e-06)
            term = jnp.tanh(0.5 * math.sqrt(length) * (lagged * scale_pair))
            total = term if total is None else total + term
        return total

    def wait_rec(target, skip):
        def one(column):
            slot = target * n_col + column
            if not skip:
                rec_copy(slot, slot).wait_recv()
        for column in range(n_col):
            one(column)

    def sum_copy(other, slot):
        return pltpu.make_async_remote_copy(
            src_ref=sent.at[other], dst_ref=landed.at[slot],
            send_sem=sum_send.at[other], recv_sem=sum_recv.at[slot],
            device_id={"row": other}, device_id_type=MESH,
        )

    def send_sum(step):
        shift = n_row // 2 + step
        shift = shift + (shift >= n_row) if isinstance(shift, int) else jnp.where(
            shift >= n_row, shift + 1, shift
        )
        target = lax.rem(row + shift, n_row)
        wait_rec(target, False)
        sent[target] = terms_for(target).astype(jnp.bfloat16)
        sum_copy(target, row).start()

    steps(n_row - 1, send_sum)

    for step in range(n_col - 1):
        slot = row * n_col + lax.rem(col + step + 1, n_col)
        rec_copy(slot, slot).wait_recv()
    fetch_stacks.wait()
    own_sum[...] = stacks_ref[...] + terms_for(row)

    def add_sum(step):
        other = lax.rem(row + n_row // 2 + step + (step + n_row // 2 >= n_row), n_row)
        sum_copy(other, other).wait_recv()
        own_sum[...] += landed[other].astype(jnp.float32)

    steps(n_row - 1, add_sum)
    out_ref[...] = own_sum[...]

    def sum_sent(step):
        sum_copy(lax.rem(row + step + 1, n_row), row).wait_send()

    def rec_sent(step):
        rec_copy(lax.rem(here + step + 1, n_row * n_col), here).wait_send()

    steps(n_row - 1, sum_sent)
    steps(n_row * n_col - 1, rec_sent)


def shards(n_row, n_col, src_raw, block_owner, chan_order, rec_raw, fir_taps, stacks):
    windows, per_device, length = rec_raw.shape
    block, columns = stacks.shape
    taps = fir_taps.shape[0]
    reach = OUT_TILE + 2 * LANES
    lags = columns // (n_col * per_device)
    devices = n_row * n_col
    tiles = length // LANES
    rec_rows = windows * per_device * tiles
    block_owner = block_owner.T
    rec_raw = jnp.transpose(rec_raw, (1, 0, 2))
    hbm = pl.BlockSpec(memory_space=pltpu.HBM)
    return pl.pallas_call(
        functools.partial(kernel, n_row, n_col, (taps - 1) // 2, lags),
        out_shape=jax.ShapeDtypeStruct(stacks.shape, stacks.dtype),
        in_specs=[hbm] * 6,
        out_specs=pl.BlockSpec(memory_space=pltpu.VMEM),
        scratch_shapes=[
            pltpu.VMEM(block_owner.shape, block_owner.dtype),
            pltpu.VMEM(chan_order.shape, chan_order.dtype),
            pltpu.VMEM((taps,), fir_taps.dtype),
            pltpu.VMEM(rec_raw.shape, rec_raw.dtype),
            pltpu.VMEM(src_raw.shape, src_raw.dtype),
            pltpu.VMEM(stacks.shape, stacks.dtype),
            pltpu.VMEM((1, reach), jnp.float32),
            pltpu.VMEM((windows * block, length + 2 * LANES), jnp.bfloat16),
            pltpu.VMEM((windows * block, length), jnp.bfloat16),
            pltpu.VMEM((-(-windows * per_device // 16) * 16, length + 2 * LANES), jnp.float32),
            pltpu.VMEM((rec_rows, LANES), jnp.float32),
            pltpu.VMEM((devices, rec_rows, LANES), jnp.bfloat16),
            pltpu.VMEM((windows, columns, length), jnp.bfloat16),
            pltpu.VMEM((block, columns), jnp.float32),
            pltpu.VMEM((n_row, block, columns), jnp.bfloat16),
            pltpu.VMEM((n_row, block, columns), jnp.bfloat16),
            pltpu.SemaphoreType.DMA((devices,)),
            pltpu.SemaphoreType.DMA((devices,)),
            pltpu.SemaphoreType.DMA((n_row,)),
            pltpu.SemaphoreType.DMA((n_row,)),
            pltpu.SemaphoreType.DMA((6,)),
        ],
        compiler_params=pltpu.CompilerParams(
            collective_id=0, has_side_effects=True, vmem_limit_bytes=60 * 1024 * 1024
        ),
        cost_estimate=pl.CostEstimate(
            flops=2 * windows * block * length * columns * n_row,
            transcendentals=2 * windows * block * columns * n_row,
            bytes_accessed=2 * windows * block * length + 8 * block * columns,
        ),
    )(block_owner, chan_order, fir_taps, rec_raw, src_raw, stacks)


def solution(mesh):
    in_specs = (
        P(("grp", "row"), None, "col", None),
        P("grp", "col"),
        P("grp", "col", None),
        P("grp", ("row", "col"), None),
        P(),
        P(("grp", "col"), "row"),
    )
    out_specs = P(("grp", "col"), "row")
    body = functools.partial(shards, mesh.shape["row"], mesh.shape["col"])
    return jax.shard_map(body, mesh=mesh, in_specs=in_specs, out_specs=out_specs, check_vma=False)
```

```python
import functools
import math

import jax
import jax.numpy as jnp
from jax import lax
from jax.experimental import pallas as pl
from jax.experimental.pallas import tpu as pltpu
from jax.sharding import PartitionSpec as P

MESH = pl.DeviceIdType.MESH
LANES = 128
OUT_TILE = 256
NT = (((1,), (1,)), ((), ()))
TN = (((0,), (0,)), ((), ()))


def steps(count, body):
    if count <= 4:
        for index in range(count):
            body(index)
    else:
        pl.loop(0, count)(body)


def kernel(
    n_row, n_col, half_taps, lags,
    owner_hbm, order_hbm, taps_hbm, rec_hbm, src_hbm, stacks_hbm,
    out_ref,
    owner_ref, order_ref, taps_ref, rec_ref, src_ref, stacks_ref, taps_row, padded, sources, rec_padded, rec_block, rec_all, hankel, own_sum, sent, landed,
    rec_send, rec_recv, sum_send, sum_recv, load_sem,
):
    row, col = lax.axis_index("row"), lax.axis_index("col")
    here = row * n_col + col
    per_device, windows, length = rec_ref.shape
    block = src_ref.shape[2]
    half_lags = lags // 2
    tiles = length // LANES
    out_tiles = length // OUT_TILE
    reach = OUT_TILE + 2 * LANES

    fetched = [
        pltpu.make_async_copy(source, target, load_sem.at[index])
        for index, (source, target) in enumerate([
            (taps_hbm, taps_ref), (rec_hbm, rec_ref), (src_hbm, src_ref),
            (order_hbm, order_ref), (owner_hbm, owner_ref), (stacks_hbm, stacks_ref),
        ])
    ]
    for copy in fetched:
        copy.start()
    fetch_taps, fetch_rec, fetch_src, fetch_order, fetch_owner, fetch_stacks = fetched

    barrier = pltpu.get_barrier_semaphore()

    def greet(step):
        other = lax.rem(here + step + 1, n_row * n_col)
        pl.semaphore_signal(
            barrier, inc=1,
            device_id={"row": other // n_col, "col": lax.rem(other, n_col)},
            device_id_type=MESH,
        )

    steps(n_row * n_col - 1, greet)

    taps_row[...] = jnp.zeros_like(taps_row)
    fetch_taps.wait()
    taps_row[:, : taps_ref.shape[0]] = taps_ref[...].astype(jnp.float32).reshape((1, -1))
    band = pltpu.roll(
        jnp.broadcast_to(taps_row[...], (OUT_TILE, reach)),
        LANES - half_taps, axis=1, stride=1, stride_axis=0,
    ).astype(jnp.bfloat16)
    flip_row = lax.broadcasted_iota(jnp.int32, (OUT_TILE, OUT_TILE), 0)
    flip_col = lax.broadcasted_iota(jnp.int32, (OUT_TILE, OUT_TILE), 1)
    flip = jnp.where(flip_row + flip_col == OUT_TILE - 1, 1.0, 0.0).astype(jnp.bfloat16)
    band = jnp.dot(flip, band, preferred_element_type=jnp.float32).astype(jnp.bfloat16)

    rec_padded[...] = jnp.zeros_like(rec_padded)
    fetch_rec.wait()
    for window in range(windows):
        for index in range(per_device):
            at = window * per_device + index
            rec_padded[at : at + 1, LANES : LANES + length] = rec_ref[
                index, window : window + 1
            ].astype(jnp.float32)
    for tile in range(out_tiles):
        taken = rec_padded[:, tile * OUT_TILE : tile * OUT_TILE + reach].astype(jnp.bfloat16)
        made = lax.dot_general(taken, band, NT, preferred_element_type=jnp.float32)
        for part in range(OUT_TILE // LANES):
            place = (out_tiles - 1 - tile) * (OUT_TILE // LANES) + part
            for at in range(windows * per_device):
                rec_block[at * tiles + place : at * tiles + place + 1, :] = made[
                    at : at + 1, part * LANES : (part + 1) * LANES
                ]
    rec_all[here] = rec_block[...].astype(jnp.bfloat16)

    pl.semaphore_wait(barrier, n_row * n_col - 1)

    def rec_copy(other, slot):
        return pltpu.make_async_remote_copy(
            src_ref=rec_all.at[slot], dst_ref=rec_all.at[slot],
            send_sem=rec_send.at[other], recv_sem=rec_recv.at[slot],
            device_id={"row": other // n_col, "col": lax.rem(other, n_col)},
            device_id_type=MESH,
        )

    def send_rec(step):
        rec_copy(lax.rem(here + step + 1, n_row * n_col), here).start()

    steps(n_row * n_col - 1, send_rec)

    padded[:, :LANES] = jnp.zeros((windows * block, LANES), jnp.bfloat16)
    padded[:, LANES + length :] = jnp.zeros((windows * block, LANES), jnp.bfloat16)
    fetch_src.wait()
    fetch_order.wait()
    fetch_owner.wait()
    for window in range(windows):
        position = lax.broadcasted_iota(jnp.int32, (block, block), 0)
        wanted = jnp.where(
            jnp.broadcast_to(owner_ref[:, window : window + 1], (1, block)) == row,
            order_ref[window], -1,
        )
        chosen = jnp.where(position == wanted, 1.0, 0.0).astype(jnp.bfloat16)
        padded[window * block : (window + 1) * block, LANES : LANES + length] = lax.dot_general(
            chosen, src_ref[0, window], TN, preferred_element_type=jnp.float32
        ).astype(jnp.bfloat16)
    src_energy = jnp.zeros((windows * block, 1), jnp.float32)
    for tile in range(out_tiles):
        made = lax.dot_general(
            padded[:, tile * OUT_TILE : tile * OUT_TILE + reach], band, NT,
            preferred_element_type=jnp.float32,
        ).astype(jnp.bfloat16)
        place = (out_tiles - 1 - tile) * OUT_TILE
        sources[:, place : place + OUT_TILE] = made
        src_energy += jnp.sum(jnp.square(made.astype(jnp.float32)), axis=1, keepdims=True)

    lag = lax.broadcasted_iota(jnp.int32, (half_lags, LANES), 0)
    lane = lax.broadcasted_iota(jnp.int32, (half_lags, LANES), 1)
    from_tile = lane < LANES - half_lags + lag
    from_tile_late = lane >= lag
    nothing = jnp.zeros((lags, LANES), jnp.float32)

    def terms_for(target):
        total = None
        for window in range(windows):
            energies = []
            for column in range(n_col):
                for index in range(per_device):
                    first = (window * per_device + index) * tiles
                    trace = rec_all[target * n_col + column].astype(jnp.float32)[
                        first : first + tiles, :
                    ]
                    energy = jnp.sum(
                        jnp.sum(jnp.square(trace), axis=0, keepdims=True), axis=1, keepdims=True
                    )
                    energies.append(jnp.broadcast_to(energy, (1, lags)))
                    turned = [
                        pltpu.roll(
                            jnp.broadcast_to(trace[tile : tile + 1, :], (lags, LANES)),
                            LANES - half_lags, axis=1, stride=1, stride_axis=0,
                        )
                        for tile in range(tiles)
                    ]
                    turned = [nothing] + turned + [nothing]
                    base = (column * per_device + index) * lags
                    for tile in range(tiles):
                        columns = slice(tile * LANES, (tile + 1) * LANES)
                        hankel[window, base : base + half_lags, columns] = jnp.where(
                            from_tile, turned[tile + 1][:half_lags], turned[tile + 2][:half_lags]
                        ).astype(jnp.bfloat16)
                        hankel[window, base + half_lags : base + lags, columns] = jnp.where(
                            from_tile_late, turned[tile + 1][half_lags:], turned[tile][half_lags:]
                        ).astype(jnp.bfloat16)
            rec_energy = jnp.concatenate(energies, axis=1)
            rows = slice(window * block, (window + 1) * block)
            lagged = lax.dot_general(
                sources[rows, :], hankel[window], NT, preferred_element_type=jnp.float32
            )
            scale_pair = lax.rsqrt(src_energy[rows] * rec_energy + 1e-06)
            term = jnp.tanh(0.5 * math.sqrt(length) * (lagged * scale_pair))
            total = term if total is None else total + term
        return total

    def wait_rec(target, skip):
        def one(column):
            slot = target * n_col + column
            if not skip:
                rec_copy(slot, slot).wait_recv()
        for column in range(n_col):
            one(column)

    def sum_copy(other, slot):
        return pltpu.make_async_remote_copy(
            src_ref=sent.at[other], dst_ref=landed.at[slot],
            send_sem=sum_send.at[other], recv_sem=sum_recv.at[slot],
            device_id={"row": other}, device_id_type=MESH,
        )

    def send_sum(step):
        shift = n_row // 2 + step
        shift = shift + (shift >= n_row) if isinstance(shift, int) else jnp.where(
            shift >= n_row, shift + 1, shift
        )
        target = lax.rem(row + shift, n_row)
        wait_rec(target, False)
        sent[target] = terms_for(target).astype(jnp.bfloat16)
        sum_copy(target, row).start()

    steps(n_row - 1, send_sum)

    for step in range(n_col - 1):
        slot = row * n_col + lax.rem(col + step + 1, n_col)
        rec_copy(slot, slot).wait_recv()
    fetch_stacks.wait()
    own_sum[...] = stacks_ref[...] + terms_for(row)

    def add_sum(step):
        other = lax.rem(row + n_row // 2 + step + (step + n_row // 2 >= n_row), n_row)
        sum_copy(other, other).wait_recv()
        own_sum[...] += landed[other].astype(jnp.float32)

    steps(n_row - 1, add_sum)
    out_ref[...] = own_sum[...]

    def sum_sent(step):
        sum_copy(lax.rem(row + step + 1, n_row), row).wait_send()

    def rec_sent(step):
        rec_copy(lax.rem(here + step + 1, n_row * n_col), here).wait_send()

    steps(n_row - 1, sum_sent)
    steps(n_row * n_col - 1, rec_sent)


def shards(n_row, n_col, src_raw, block_owner, chan_order, rec_raw, fir_taps, stacks):
    windows, per_device, length = rec_raw.shape
    block, columns = stacks.shape
    taps = fir_taps.shape[0]
    reach = OUT_TILE + 2 * LANES
    lags = columns // (n_col * per_device)
    devices = n_row * n_col
    tiles = length // LANES
    rec_rows = windows * per_device * tiles
    block_owner = block_owner.T
    rec_raw = jnp.transpose(rec_raw, (1, 0, 2))
    hbm = pl.BlockSpec(memory_space=pltpu.HBM)
    return pl.pallas_call(
        functools.partial(kernel, n_row, n_col, (taps - 1) // 2, lags),
        out_shape=jax.ShapeDtypeStruct(stacks.shape, stacks.dtype),
        in_specs=[hbm] * 6,
        out_specs=pl.BlockSpec(memory_space=pltpu.VMEM),
        scratch_shapes=[
            pltpu.VMEM(block_owner.shape, block_owner.dtype),
            pltpu.VMEM(chan_order.shape, chan_order.dtype),
            pltpu.VMEM((taps,), fir_taps.dtype),
            pltpu.VMEM(rec_raw.shape, rec_raw.dtype),
            pltpu.VMEM(src_raw.shape, src_raw.dtype),
            pltpu.VMEM(stacks.shape, stacks.dtype),
            pltpu.VMEM((1, reach), jnp.float32),
            pltpu.VMEM((windows * block, length + 2 * LANES), jnp.bfloat16),
            pltpu.VMEM((windows * block, length), jnp.bfloat16),
            pltpu.VMEM((-(-windows * per_device // 16) * 16, length + 2 * LANES), jnp.float32),
            pltpu.VMEM((rec_rows, LANES), jnp.float32),
            pltpu.VMEM((devices, rec_rows, LANES), jnp.bfloat16),
            pltpu.VMEM((windows, columns, length), jnp.bfloat16),
            pltpu.VMEM((block, columns), jnp.float32),
            pltpu.VMEM((n_row, block, columns), jnp.bfloat16),
            pltpu.VMEM((n_row, block, columns), jnp.bfloat16),
            pltpu.SemaphoreType.DMA((devices,)),
            pltpu.SemaphoreType.DMA((devices,)),
            pltpu.SemaphoreType.DMA((n_row,)),
            pltpu.SemaphoreType.DMA((n_row,)),
            pltpu.SemaphoreType.DMA((6,)),
        ],
        compiler_params=pltpu.CompilerParams(
            collective_id=0, has_side_effects=True, vmem_limit_bytes=32 * 1024 * 1024
        ),
        cost_estimate=pl.CostEstimate(
            flops=2 * windows * block * length * columns * n_row,
            transcendentals=2 * windows * block * columns * n_row,
            bytes_accessed=2 * windows * block * length + 8 * block * columns,
        ),
    )(*(
        pltpu.with_memory_space_constraint(operand, pltpu.HBM)
        for operand in (block_owner, chan_order, fir_taps, rec_raw, src_raw, stacks)
    ))


def solution(mesh):
    in_specs = (
        P(("grp", "row"), None, "col", None),
        P("grp", "col"),
        P("grp", "col", None),
        P("grp", ("row", "col"), None),
        P(),
        P(("grp", "col"), "row"),
    )
    out_specs = P(("grp", "col"), "row")
    body = functools.partial(shards, mesh.shape["row"], mesh.shape["col"])
    return jax.shard_map(body, mesh=mesh, in_specs=in_specs, out_specs=out_specs, check_vma=False)
```

```python
import functools
import math

import jax
import jax.numpy as jnp
from jax import lax
from jax.experimental import pallas as pl
from jax.experimental.pallas import tpu as pltpu
from jax.sharding import PartitionSpec as P

MESH = pl.DeviceIdType.MESH
LANES = 128
OUT_TILE = 256
NT = (((1,), (1,)), ((), ()))
TN = (((0,), (0,)), ((), ()))


def steps(count, body):
    if count <= 16:
        for index in range(count):
            body(index)
    else:
        pl.loop(0, count)(body)


def kernel(
    n_row, n_col, half_taps, lags,
    owner_hbm, order_hbm, taps_hbm, rec_hbm, src_hbm, stacks_hbm,
    out_ref,
    owner_ref, order_ref, taps_ref, rec_ref, src_ref, stacks_ref, taps_row, padded, sources, rec_padded, rec_block, rec_all, hankel, sent, landed,
    rec_send, rec_recv, sum_send, sum_recv, load_sem,
):
    row, col = lax.axis_index("row"), lax.axis_index("col")
    here = row * n_col + col
    per_device, windows, length = rec_ref.shape
    block = src_ref.shape[2]
    half_lags = lags // 2
    tiles = length // LANES
    out_tiles = length // OUT_TILE
    reach = OUT_TILE + 2 * LANES

    fetched = [
        pltpu.make_async_copy(source, target, load_sem.at[index])
        for index, (source, target) in enumerate([
            (taps_hbm, taps_ref), (rec_hbm, rec_ref), (src_hbm, src_ref),
            (order_hbm, order_ref), (owner_hbm, owner_ref), (stacks_hbm, stacks_ref),
        ])
    ]
    for copy in fetched:
        copy.start()
    fetch_taps, fetch_rec, fetch_src, fetch_order, fetch_owner, fetch_stacks = fetched

    barrier = pltpu.get_barrier_semaphore()

    def greet(step):
        other = lax.rem(here + step + 1, n_row * n_col)
        pl.semaphore_signal(
            barrier, inc=1,
            device_id={"row": other // n_col, "col": lax.rem(other, n_col)},
            device_id_type=MESH,
        )

    steps(n_row * n_col - 1, greet)

    flip_row = lax.broadcasted_iota(jnp.int32, (LANES, LANES), 0)
    flip_col = lax.broadcasted_iota(jnp.int32, (LANES, LANES), 1)
    flip = jnp.where(flip_row + flip_col == LANES - 1, 1.0, 0.0).astype(jnp.bfloat16)
    empty = jnp.zeros((LANES, LANES), jnp.bfloat16)
    taps_row[...] = jnp.zeros_like(taps_row)
    rec_padded[...] = jnp.zeros_like(rec_padded)
    padded[:, :LANES] = jnp.zeros((windows * block, LANES), jnp.bfloat16)
    padded[:, LANES + length :] = jnp.zeros((windows * block, LANES), jnp.bfloat16)
    fetch_taps.wait()
    taps_row[:, : taps_ref.shape[0]] = taps_ref[...].astype(jnp.float32).reshape((1, -1))
    band = pltpu.roll(
        jnp.broadcast_to(taps_row[...], (LANES, 3 * LANES)),
        LANES - half_taps, axis=1, stride=1, stride_axis=0,
    ).astype(jnp.bfloat16)
    band = jnp.dot(flip, band, preferred_element_type=jnp.float32).astype(jnp.bfloat16)
    band = jnp.concatenate(
        [jnp.concatenate([empty, band], axis=1), jnp.concatenate([band, empty], axis=1)], axis=0
    )

    fetch_rec.wait()
    for window in range(windows):
        for index in range(per_device):
            at = window * per_device + index
            rec_padded[at : at + 1, LANES : LANES + length] = rec_ref[
                index, window : window + 1
            ].astype(jnp.float32)
    for tile in range(out_tiles):
        taken = rec_padded[:, tile * OUT_TILE : tile * OUT_TILE + reach].astype(jnp.bfloat16)
        made = lax.dot_general(taken, band, NT, preferred_element_type=jnp.float32)
        for part in range(OUT_TILE // LANES):
            place = (out_tiles - 1 - tile) * (OUT_TILE // LANES) + part
            for at in range(windows * per_device):
                rec_block[at * tiles + place : at * tiles + place + 1, :] = made[
                    at : at + 1, part * LANES : (part + 1) * LANES
                ]
    rec_all[here] = rec_block[...].astype(jnp.bfloat16)

    pl.semaphore_wait(barrier, n_row * n_col - 1)

    def rec_copy(other, slot):
        return pltpu.make_async_remote_copy(
            src_ref=rec_all.at[slot], dst_ref=rec_all.at[slot],
            send_sem=rec_send.at[other], recv_sem=rec_recv.at[slot],
            device_id={"row": other // n_col, "col": lax.rem(other, n_col)},
            device_id_type=MESH,
        )

    def send_rec(step):
        first = (n_row // 2) * n_col
        if isinstance(step, int):
            other = lax.rem(here + first + step + (step + first >= n_row * n_col), n_row * n_col)
        else:
            other = lax.rem(
                here + jnp.where(step + first >= n_row * n_col, step + first + 1, step + first),
                n_row * n_col,
            )
        rec_copy(other, here).start()

    steps(n_row * n_col - 1, send_rec)

    fetch_src.wait()
    fetch_order.wait()
    fetch_owner.wait()
    for window in range(windows):
        position = lax.broadcasted_iota(jnp.int32, (block, block), 0)
        wanted = jnp.where(
            jnp.broadcast_to(owner_ref[:, window : window + 1], (1, block)) == row,
            order_ref[window], -1,
        )
        chosen = jnp.where(position == wanted, 1.0, 0.0).astype(jnp.bfloat16)
        padded[window * block : (window + 1) * block, LANES : LANES + length] = lax.dot_general(
            chosen, src_ref[0, window], TN, preferred_element_type=jnp.float32
        ).astype(jnp.bfloat16)
    src_energy = jnp.zeros((windows * block, 1), jnp.float32)
    for tile in range(out_tiles):
        made = lax.dot_general(
            padded[:, tile * OUT_TILE : tile * OUT_TILE + reach], band, NT,
            preferred_element_type=jnp.float32,
        ).astype(jnp.bfloat16)
        place = (out_tiles - 1 - tile) * OUT_TILE
        sources[:, place : place + OUT_TILE] = made
        src_energy += jnp.sum(jnp.square(made.astype(jnp.float32)), axis=1, keepdims=True)

    lag = lax.broadcasted_iota(jnp.int32, (half_lags, LANES), 0)
    lane = lax.broadcasted_iota(jnp.int32, (half_lags, LANES), 1)
    from_tile = lane < LANES - half_lags + lag
    from_tile_late = lane >= lag
    nothing = jnp.zeros((lags, LANES), jnp.float32)

    def terms_for(target, slot):
        total = None
        for window in range(windows):
            energies = []
            for column in range(n_col):
                for index in range(per_device):
                    first = (window * per_device + index) * tiles
                    trace = rec_all[target * n_col + column].astype(jnp.float32)[
                        first : first + tiles, :
                    ]
                    energy = jnp.sum(
                        jnp.sum(jnp.square(trace), axis=0, keepdims=True), axis=1, keepdims=True
                    )
                    energies.append(jnp.broadcast_to(energy, (1, lags)))
                    turned = [
                        pltpu.roll(
                            jnp.broadcast_to(trace[tile : tile + 1, :], (lags, LANES)),
                            LANES - half_lags, axis=1, stride=1, stride_axis=0,
                        )
                        for tile in range(tiles)
                    ]
                    turned = [nothing] + turned + [nothing]
                    base = (column * per_device + index) * lags
                    for tile in range(tiles):
                        columns = slice(tile * LANES, (tile + 1) * LANES)
                        hankel[slot, window, base : base + half_lags, columns] = jnp.where(
                            from_tile, turned[tile + 1][:half_lags], turned[tile + 2][:half_lags]
                        ).astype(jnp.bfloat16)
                        hankel[slot, window, base + half_lags : base + lags, columns] = jnp.where(
                            from_tile_late, turned[tile + 1][half_lags:], turned[tile][half_lags:]
                        ).astype(jnp.bfloat16)
            rec_energy = jnp.concatenate(energies, axis=1)
            rows = slice(window * block, (window + 1) * block)
            lagged = lax.dot_general(
                sources[rows, :], hankel[slot, window], NT, preferred_element_type=jnp.float32
            )
            scale_pair = lax.rsqrt(src_energy[rows] * rec_energy + 1e-06)
            term = jnp.tanh(0.5 * math.sqrt(length) * (lagged * scale_pair))
            total = term if total is None else total + term
        return total

    def wait_rec(target, skip):
        def one(column):
            slot = target * n_col + column
            if not skip:
                rec_copy(slot, slot).wait_recv()
        for column in range(n_col):
            one(column)

    def sum_copy(other, slot):
        return pltpu.make_async_remote_copy(
            src_ref=sent.at[other], dst_ref=landed.at[slot],
            send_sem=sum_send.at[other], recv_sem=sum_recv.at[slot],
            device_id={"row": other}, device_id_type=MESH,
        )

    def send_sum(step):
        shift = n_row // 2 + step
        shift = shift + (shift >= n_row) if isinstance(shift, int) else jnp.where(
            shift >= n_row, shift + 1, shift
        )
        target = lax.rem(row + shift, n_row)
        wait_rec(target, False)
        sent[target] = terms_for(target, step % 2).astype(jnp.bfloat16)
        sum_copy(target, row).start()

    steps(n_row - 1, send_sum)

    for step in range(n_col - 1):
        slot = row * n_col + lax.rem(col + step + 1, n_col)
        rec_copy(slot, slot).wait_recv()
    fetch_stacks.wait()
    out_ref[...] = stacks_ref[...] + terms_for(row, (n_row - 1) % 2)

    def add_sum(step):
        other = lax.rem(row + n_row // 2 + step + (step + n_row // 2 >= n_row), n_row)
        sum_copy(other, other).wait_recv()
        out_ref[...] += landed[other].astype(jnp.float32)

    steps(n_row - 1, add_sum)

    def sum_sent(step):
        sum_copy(lax.rem(row + step + 1, n_row), row).wait_send()

    def rec_sent(step):
        rec_copy(lax.rem(here + step + 1, n_row * n_col), here).wait_send()

    steps(n_row - 1, sum_sent)
    steps(n_row * n_col - 1, rec_sent)


def shards(n_row, n_col, src_raw, block_owner, chan_order, rec_raw, fir_taps, stacks):
    windows, per_device, length = rec_raw.shape
    block, columns = stacks.shape
    taps = fir_taps.shape[0]
    lags = columns // (n_col * per_device)
    devices = n_row * n_col
    tiles = length // LANES
    rec_rows = windows * per_device * tiles
    block_owner = block_owner.T
    rec_raw = jnp.transpose(rec_raw, (1, 0, 2))
    hbm = pl.BlockSpec(memory_space=pltpu.HBM)
    return pl.pallas_call(
        functools.partial(kernel, n_row, n_col, (taps - 1) // 2, lags),
        out_shape=jax.ShapeDtypeStruct(stacks.shape, stacks.dtype),
        in_specs=[hbm] * 6,
        out_specs=pl.BlockSpec(memory_space=pltpu.VMEM),
        scratch_shapes=[
            pltpu.VMEM(block_owner.shape, block_owner.dtype),
            pltpu.VMEM(chan_order.shape, chan_order.dtype),
            pltpu.VMEM((taps,), fir_taps.dtype),
            pltpu.VMEM(rec_raw.shape, rec_raw.dtype),
            pltpu.VMEM(src_raw.shape, src_raw.dtype),
            pltpu.VMEM(stacks.shape, stacks.dtype),
            pltpu.VMEM((1, 3 * LANES), jnp.float32),
            pltpu.VMEM((windows * block, length + 2 * LANES), jnp.bfloat16),
            pltpu.VMEM((windows * block, length), jnp.bfloat16),
            pltpu.VMEM((-(-windows * per_device // 16) * 16, length + 2 * LANES), jnp.float32),
            pltpu.VMEM((rec_rows, LANES), jnp.float32),
            pltpu.VMEM((devices, rec_rows, LANES), jnp.bfloat16),
            pltpu.VMEM((2, windows, columns, length), jnp.bfloat16),
            pltpu.VMEM((n_row, block, columns), jnp.bfloat16),
            pltpu.VMEM((n_row, block, columns), jnp.bfloat16),
            pltpu.SemaphoreType.DMA((devices,)),
            pltpu.SemaphoreType.DMA((devices,)),
            pltpu.SemaphoreType.DMA((n_row,)),
            pltpu.SemaphoreType.DMA((n_row,)),
            pltpu.SemaphoreType.DMA((6,)),
        ],
        compiler_params=pltpu.CompilerParams(
            collective_id=0, has_side_effects=True, vmem_limit_bytes=32 * 1024 * 1024
        ),
        cost_estimate=pl.CostEstimate(
            flops=2 * windows * block * length * columns * n_row,
            transcendentals=2 * windows * block * columns * n_row,
            bytes_accessed=2 * windows * block * length + 8 * block * columns,
        ),
    )(*(
        pltpu.with_memory_space_constraint(operand, pltpu.HBM)
        for operand in (block_owner, chan_order, fir_taps, rec_raw, src_raw, stacks)
    ))


def solution(mesh):
    in_specs = (
        P(("grp", "row"), None, "col", None),
        P("grp", "col"),
        P("grp", "col", None),
        P("grp", ("row", "col"), None),
        P(),
        P(("grp", "col"), "row"),
    )
    out_specs = P(("grp", "col"), "row")
    body = functools.partial(shards, mesh.shape["row"], mesh.shape["col"])
    return jax.shard_map(body, mesh=mesh, in_specs=in_specs, out_specs=out_specs, check_vma=False)
```

```python
import functools
import math

import jax
import jax.numpy as jnp
from jax import lax
from jax.experimental import pallas as pl
from jax.experimental.pallas import tpu as pltpu
from jax.sharding import PartitionSpec as P

MESH = pl.DeviceIdType.MESH
LANES = 128
OUT_TILE = 256
NT = (((1,), (1,)), ((), ()))
TN = (((0,), (0,)), ((), ()))


def steps(count, body):
    if count <= 16:
        for index in range(count):
            body(index)
    else:
        pl.loop(0, count)(body)


def kernel(
    n_row, n_col, half_taps, lags,
    owner_hbm, order_hbm, taps_hbm, rec_hbm, src_hbm, stacks_hbm,
    out_ref,
    owner_ref, order_ref, taps_ref, rec_ref, src_ref, stacks_ref, taps_row, padded, sources, rec_padded, rec_block, rec_all, hankel, sent, landed,
    rec_send, rec_recv, sum_send, sum_recv, load_sem,
):
    row, col = lax.axis_index("row"), lax.axis_index("col")
    here = row * n_col + col
    per_device, windows, length = rec_ref.shape
    block = src_ref.shape[2]
    half_lags = lags // 2
    tiles = length // LANES
    out_tiles = length // OUT_TILE
    reach = OUT_TILE + 2 * LANES

    fetched = [
        pltpu.make_async_copy(source, target, load_sem.at[index])
        for index, (source, target) in enumerate([
            (taps_hbm, taps_ref), (rec_hbm, rec_ref), (src_hbm, src_ref),
            (order_hbm, order_ref), (owner_hbm, owner_ref), (stacks_hbm, stacks_ref),
        ])
    ]
    for copy in fetched:
        copy.start()
    fetch_taps, fetch_rec, fetch_src, fetch_order, fetch_owner, fetch_stacks = fetched

    barrier = pltpu.get_barrier_semaphore()

    def greet(step):
        other = lax.rem(here + step + 1, n_row * n_col)
        pl.semaphore_signal(
            barrier, inc=1,
            device_id={"row": other // n_col, "col": lax.rem(other, n_col)},
            device_id_type=MESH,
        )

    steps(n_row * n_col - 1, greet)

    flip_row = lax.broadcasted_iota(jnp.int32, (LANES, LANES), 0)
    flip_col = lax.broadcasted_iota(jnp.int32, (LANES, LANES), 1)
    flip = jnp.where(flip_row + flip_col == LANES - 1, 1.0, 0.0).astype(jnp.bfloat16)
    empty = jnp.zeros((LANES, LANES), jnp.bfloat16)
    taps_row[...] = jnp.zeros_like(taps_row)
    rec_padded[...] = jnp.zeros_like(rec_padded)
    padded[:, :LANES] = jnp.zeros((windows * block, LANES), jnp.bfloat16)
    padded[:, LANES + length :] = jnp.zeros((windows * block, LANES), jnp.bfloat16)
    fetch_taps.wait()
    taps_row[:, : taps_ref.shape[0]] = taps_ref[...].astype(jnp.float32).reshape((1, -1))
    band = pltpu.roll(
        jnp.broadcast_to(taps_row[...], (LANES, 3 * LANES)),
        LANES - half_taps, axis=1, stride=1, stride_axis=0,
    ).astype(jnp.bfloat16)
    band = jnp.dot(flip, band, preferred_element_type=jnp.float32).astype(jnp.bfloat16)
    band = jnp.concatenate(
        [jnp.concatenate([empty, band], axis=1), jnp.concatenate([band, empty], axis=1)], axis=0
    )

    fetch_rec.wait()
    for window in range(windows):
        for index in range(per_device):
            at = window * per_device + index
            rec_padded[at : at + 1, LANES : LANES + length] = rec_ref[
                index, window : window + 1
            ].astype(jnp.float32)
    for tile in range(out_tiles):
        taken = rec_padded[:, tile * OUT_TILE : tile * OUT_TILE + reach].astype(jnp.bfloat16)
        made = lax.dot_general(taken, band, NT, preferred_element_type=jnp.float32)
        for part in range(OUT_TILE // LANES):
            place = (out_tiles - 1 - tile) * (OUT_TILE // LANES) + part
            for at in range(windows * per_device):
                rec_block[at * tiles + place : at * tiles + place + 1, :] = made[
                    at : at + 1, part * LANES : (part + 1) * LANES
                ]
    rec_all[here] = rec_block[...].astype(jnp.bfloat16)

    pl.semaphore_wait(barrier, n_row * n_col - 1)

    def rec_copy(other, slot):
        return pltpu.make_async_remote_copy(
            src_ref=rec_all.at[slot], dst_ref=rec_all.at[slot],
            send_sem=rec_send.at[other], recv_sem=rec_recv.at[slot],
            device_id={"row": other // n_col, "col": lax.rem(other, n_col)},
            device_id_type=MESH,
        )

    def send_rec(step):
        other = lax.rem(here + n_row * n_col - 1 - step, n_row * n_col)
        rec_copy(other, here).start()

    steps(n_row * n_col - 1, send_rec)

    fetch_src.wait()
    fetch_order.wait()
    fetch_owner.wait()
    for window in range(windows):
        position = lax.broadcasted_iota(jnp.int32, (block, block), 0)
        wanted = jnp.where(
            jnp.broadcast_to(owner_ref[:, window : window + 1], (1, block)) == row,
            order_ref[window], -1,
        )
        chosen = jnp.where(position == wanted, 1.0, 0.0).astype(jnp.bfloat16)
        padded[window * block : (window + 1) * block, LANES : LANES + length] = lax.dot_general(
            chosen, src_ref[0, window], TN, preferred_element_type=jnp.float32
        ).astype(jnp.bfloat16)
    src_energy = jnp.zeros((windows * block, 1), jnp.float32)
    for tile in range(out_tiles):
        made = lax.dot_general(
            padded[:, tile * OUT_TILE : tile * OUT_TILE + reach], band, NT,
            preferred_element_type=jnp.float32,
        ).astype(jnp.bfloat16)
        place = (out_tiles - 1 - tile) * OUT_TILE
        sources[:, place : place + OUT_TILE] = made
        src_energy += jnp.sum(jnp.square(made.astype(jnp.float32)), axis=1, keepdims=True)

    lag = lax.broadcasted_iota(jnp.int32, (half_lags, LANES), 0)
    lane = lax.broadcasted_iota(jnp.int32, (half_lags, LANES), 1)
    from_tile = lane < LANES - half_lags + lag
    from_tile_late = lane >= lag
    nothing = jnp.zeros((lags, LANES), jnp.float32)

    def terms_for(target, slot):
        total = None
        for window in range(windows):
            energies = []
            for column in range(n_col):
                for index in range(per_device):
                    first = (window * per_device + index) * tiles
                    trace = rec_all[target * n_col + column].astype(jnp.float32)[
                        first : first + tiles, :
                    ]
                    energy = jnp.sum(
                        jnp.sum(jnp.square(trace), axis=0, keepdims=True), axis=1, keepdims=True
                    )
                    energies.append(jnp.broadcast_to(energy, (1, lags)))
                    turned = [
                        pltpu.roll(
                            jnp.broadcast_to(trace[tile : tile + 1, :], (lags, LANES)),
                            LANES - half_lags, axis=1, stride=1, stride_axis=0,
                        )
                        for tile in range(tiles)
                    ]
                    turned = [nothing] + turned + [nothing]
                    base = (column * per_device + index) * lags
                    for tile in range(tiles):
                        columns = slice(tile * LANES, (tile + 1) * LANES)
                        hankel[slot, window, base : base + half_lags, columns] = jnp.where(
                            from_tile, turned[tile + 1][:half_lags], turned[tile + 2][:half_lags]
                        ).astype(jnp.bfloat16)
                        hankel[slot, window, base + half_lags : base + lags, columns] = jnp.where(
                            from_tile_late, turned[tile + 1][half_lags:], turned[tile][half_lags:]
                        ).astype(jnp.bfloat16)
            rec_energy = jnp.concatenate(energies, axis=1)
            rows = slice(window * block, (window + 1) * block)
            lagged = lax.dot_general(
                sources[rows, :], hankel[slot, window], NT, preferred_element_type=jnp.float32
            )
            scale_pair = lax.rsqrt(src_energy[rows] * rec_energy + 1e-06)
            term = jnp.tanh(0.5 * math.sqrt(length) * (lagged * scale_pair))
            total = term if total is None else total + term
        return total

    def wait_rec(target, skip):
        def one(column):
            slot = target * n_col + column
            if not skip:
                rec_copy(slot, slot).wait_recv()
        for column in range(n_col):
            one(column)

    def sum_copy(other, slot):
        return pltpu.make_async_remote_copy(
            src_ref=sent.at[other], dst_ref=landed.at[slot],
            send_sem=sum_send.at[other], recv_sem=sum_recv.at[slot],
            device_id={"row": other}, device_id_type=MESH,
        )

    def send_sum(step):
        target = step + jnp.where(step >= row, 1, 0)
        wait_rec(target, False)
        sent[target] = terms_for(target, step % 2).astype(jnp.bfloat16)
        sum_copy(target, row).start()

    steps(n_row - 1, send_sum)

    for step in range(n_col - 1):
        slot = row * n_col + lax.rem(col + step + 1, n_col)
        rec_copy(slot, slot).wait_recv()
    fetch_stacks.wait()
    out_ref[...] = stacks_ref[...] + terms_for(row, (n_row - 1) % 2)

    def add_sum(step):
        other = step + jnp.where(step >= row, 1, 0)
        sum_copy(other, other).wait_recv()
        out_ref[...] += landed[other].astype(jnp.float32)

    steps(n_row - 1, add_sum)

    def sum_sent(step):
        sum_copy(lax.rem(row + step + 1, n_row), row).wait_send()

    def rec_sent(step):
        rec_copy(lax.rem(here + step + 1, n_row * n_col), here).wait_send()

    steps(n_row - 1, sum_sent)
    steps(n_row * n_col - 1, rec_sent)


def shards(n_row, n_col, src_raw, block_owner, chan_order, rec_raw, fir_taps, stacks):
    windows, per_device, length = rec_raw.shape
    block, columns = stacks.shape
    taps = fir_taps.shape[0]
    lags = columns // (n_col * per_device)
    devices = n_row * n_col
    tiles = length // LANES
    rec_rows = windows * per_device * tiles
    block_owner = block_owner.T
    rec_raw = jnp.transpose(rec_raw, (1, 0, 2))
    hbm = pl.BlockSpec(memory_space=pltpu.HBM)
    return pl.pallas_call(
        functools.partial(kernel, n_row, n_col, (taps - 1) // 2, lags),
        out_shape=jax.ShapeDtypeStruct(stacks.shape, stacks.dtype),
        in_specs=[hbm] * 6,
        out_specs=pl.BlockSpec(memory_space=pltpu.VMEM),
        scratch_shapes=[
            pltpu.VMEM(block_owner.shape, block_owner.dtype),
            pltpu.VMEM(chan_order.shape, chan_order.dtype),
            pltpu.VMEM((taps,), fir_taps.dtype),
            pltpu.VMEM(rec_raw.shape, rec_raw.dtype),
            pltpu.VMEM(src_raw.shape, src_raw.dtype),
            pltpu.VMEM(stacks.shape, stacks.dtype),
            pltpu.VMEM((1, 3 * LANES), jnp.float32),
            pltpu.VMEM((windows * block, length + 2 * LANES), jnp.bfloat16),
            pltpu.VMEM((windows * block, length), jnp.bfloat16),
            pltpu.VMEM((-(-windows * per_device // 16) * 16, length + 2 * LANES), jnp.float32),
            pltpu.VMEM((rec_rows, LANES), jnp.float32),
            pltpu.VMEM((devices, rec_rows, LANES), jnp.bfloat16),
            pltpu.VMEM((2, windows, columns, length), jnp.bfloat16),
            pltpu.VMEM((n_row, block, columns), jnp.bfloat16),
            pltpu.VMEM((n_row, block, columns), jnp.bfloat16),
            pltpu.SemaphoreType.DMA((devices,)),
            pltpu.SemaphoreType.DMA((devices,)),
            pltpu.SemaphoreType.DMA((n_row,)),
            pltpu.SemaphoreType.DMA((n_row,)),
            pltpu.SemaphoreType.DMA((6,)),
        ],
        compiler_params=pltpu.CompilerParams(
            collective_id=0, has_side_effects=True, vmem_limit_bytes=32 * 1024 * 1024
        ),
        cost_estimate=pl.CostEstimate(
            flops=2 * windows * block * length * columns * n_row,
            transcendentals=2 * windows * block * columns * n_row,
            bytes_accessed=2 * windows * block * length + 8 * block * columns,
        ),
    )(*(
        pltpu.with_memory_space_constraint(operand, pltpu.HBM)
        for operand in (block_owner, chan_order, fir_taps, rec_raw, src_raw, stacks)
    ))


def solution(mesh):
    in_specs = (
        P(("grp", "row"), None, "col", None),
        P("grp", "col"),
        P("grp", "col", None),
        P("grp", ("row", "col"), None),
        P(),
        P(("grp", "col"), "row"),
    )
    out_specs = P(("grp", "col"), "row")
    body = functools.partial(shards, mesh.shape["row"], mesh.shape["col"])
    return jax.shard_map(body, mesh=mesh, in_specs=in_specs, out_specs=out_specs, check_vma=False)
```

```python
import functools
import math

import jax
import jax.numpy as jnp
from jax import lax
from jax.experimental import pallas as pl
from jax.experimental.pallas import tpu as pltpu
from jax.sharding import PartitionSpec as P

MESH = pl.DeviceIdType.MESH
LANES = 128
OUT_TILE = 256
NT = (((1,), (1,)), ((), ()))
TN = (((0,), (0,)), ((), ()))


def steps(count, body):
    if count <= 16:
        for index in range(count):
            body(index)
    else:
        pl.loop(0, count)(body)


def kernel(
    n_row, n_col, half_taps, lags,
    owner_hbm, order_hbm, taps_hbm, rec_hbm, src_hbm, stacks_hbm,
    out_ref,
    owner_ref, order_ref, taps_ref, rec_ref, src_ref, stacks_ref, taps_row, padded, sources, rec_padded, rec_block, rec_all, hankel, sent, landed,
    rec_send, rec_recv, sum_send, sum_recv, load_sem,
):
    row, col = lax.axis_index("row"), lax.axis_index("col")
    here = row * n_col + col
    per_device, windows, length = rec_ref.shape
    block = src_ref.shape[2]
    half_lags = lags // 2
    tiles = length // LANES
    out_tiles = length // OUT_TILE
    reach = OUT_TILE + 2 * LANES

    fetched = [
        pltpu.make_async_copy(source, target, load_sem.at[index])
        for index, (source, target) in enumerate([
            (taps_hbm, taps_ref), (rec_hbm, rec_ref), (src_hbm, src_ref),
            (order_hbm, order_ref), (owner_hbm, owner_ref), (stacks_hbm, stacks_ref),
        ])
    ]
    for copy in fetched:
        copy.start()
    fetch_taps, fetch_rec, fetch_src, fetch_order, fetch_owner, fetch_stacks = fetched

    barrier = pltpu.get_barrier_semaphore()

    def greet(step):
        other = lax.rem(here + step + 1, n_row * n_col)
        pl.semaphore_signal(
            barrier, inc=1,
            device_id={"row": other // n_col, "col": lax.rem(other, n_col)},
            device_id_type=MESH,
        )

    steps(n_row * n_col - 1, greet)

    flip_row = lax.broadcasted_iota(jnp.int32, (LANES, LANES), 0)
    flip_col = lax.broadcasted_iota(jnp.int32, (LANES, LANES), 1)
    flip = jnp.where(flip_row + flip_col == LANES - 1, 1.0, 0.0).astype(jnp.bfloat16)
    empty = jnp.zeros((LANES, LANES), jnp.bfloat16)
    taps_row[...] = jnp.zeros_like(taps_row)
    rec_padded[...] = jnp.zeros_like(rec_padded)
    padded[:, :LANES] = jnp.zeros((windows * block, LANES), jnp.bfloat16)
    padded[:, LANES + length :] = jnp.zeros((windows * block, LANES), jnp.bfloat16)
    fetch_taps.wait()
    taps_row[:, : taps_ref.shape[0]] = taps_ref[...].astype(jnp.float32).reshape((1, -1))
    band = pltpu.roll(
        jnp.broadcast_to(taps_row[...], (LANES, 3 * LANES)),
        LANES - half_taps, axis=1, stride=1, stride_axis=0,
    ).astype(jnp.bfloat16)
    band = jnp.dot(flip, band, preferred_element_type=jnp.float32).astype(jnp.bfloat16)
    band = jnp.concatenate(
        [jnp.concatenate([empty, band], axis=1), jnp.concatenate([band, empty], axis=1)], axis=0
    )

    fetch_rec.wait()
    for window in range(windows):
        for index in range(per_device):
            at = window * per_device + index
            rec_padded[at : at + 1, LANES : LANES + length] = rec_ref[
                index, window : window + 1
            ].astype(jnp.float32)
    for tile in range(out_tiles):
        taken = rec_padded[:, tile * OUT_TILE : tile * OUT_TILE + reach].astype(jnp.bfloat16)
        made = lax.dot_general(taken, band, NT, preferred_element_type=jnp.float32)
        for part in range(OUT_TILE // LANES):
            place = (out_tiles - 1 - tile) * (OUT_TILE // LANES) + part
            for at in range(windows * per_device):
                rec_block[at * tiles + place : at * tiles + place + 1, :] = made[
                    at : at + 1, part * LANES : (part + 1) * LANES
                ]
    rec_all[here] = rec_block[...].astype(jnp.bfloat16)

    fetch_src.wait()
    fetch_order.wait()
    fetch_owner.wait()
    for window in range(windows):
        position = lax.broadcasted_iota(jnp.int32, (block, block), 0)
        wanted = jnp.where(
            jnp.broadcast_to(owner_ref[:, window : window + 1], (1, block)) == row,
            order_ref[window], -1,
        )
        chosen = jnp.where(position == wanted, 1.0, 0.0).astype(jnp.bfloat16)
        padded[window * block : (window + 1) * block, LANES : LANES + length] = lax.dot_general(
            chosen, src_ref[0, window], TN, preferred_element_type=jnp.float32
        ).astype(jnp.bfloat16)
    src_energy = jnp.zeros((windows * block, 1), jnp.float32)
    for tile in range(out_tiles):
        made = lax.dot_general(
            padded[:, tile * OUT_TILE : tile * OUT_TILE + reach], band, NT,
            preferred_element_type=jnp.float32,
        ).astype(jnp.bfloat16)
        place = (out_tiles - 1 - tile) * OUT_TILE
        sources[:, place : place + OUT_TILE] = made
        src_energy += jnp.sum(jnp.square(made.astype(jnp.float32)), axis=1, keepdims=True)

    pl.semaphore_wait(barrier, n_row * n_col - 1)

    def rec_copy(other, slot):
        return pltpu.make_async_remote_copy(
            src_ref=rec_all.at[slot], dst_ref=rec_all.at[slot],
            send_sem=rec_send.at[other], recv_sem=rec_recv.at[slot],
            device_id={"row": other // n_col, "col": lax.rem(other, n_col)},
            device_id_type=MESH,
        )

    def send_rec(step):
        other = lax.rem(here + n_row * n_col - 1 - step, n_row * n_col)
        rec_copy(other, here).start()

    steps(n_row * n_col - 1, send_rec)

    lag = lax.broadcasted_iota(jnp.int32, (half_lags, LANES), 0)
    lane = lax.broadcasted_iota(jnp.int32, (half_lags, LANES), 1)
    from_tile = lane < LANES - half_lags + lag
    from_tile_late = lane >= lag
    nothing = jnp.zeros((lags, LANES), jnp.float32)

    def terms_for(target, slot):
        total = None
        for window in range(windows):
            energies = []
            for column in range(n_col):
                for index in range(per_device):
                    first = (window * per_device + index) * tiles
                    trace = rec_all[target * n_col + column].astype(jnp.float32)[
                        first : first + tiles, :
                    ]
                    energy = jnp.sum(
                        jnp.sum(jnp.square(trace), axis=0, keepdims=True), axis=1, keepdims=True
                    )
                    energies.append(jnp.broadcast_to(energy, (1, lags)))
                    turned = [
                        pltpu.roll(
                            jnp.broadcast_to(trace[tile : tile + 1, :], (lags, LANES)),
                            LANES - half_lags, axis=1, stride=1, stride_axis=0,
                        )
                        for tile in range(tiles)
                    ]
                    turned = [nothing] + turned + [nothing]
                    base = (column * per_device + index) * lags
                    for tile in range(tiles):
                        columns = slice(tile * LANES, (tile + 1) * LANES)
                        hankel[slot, window, base : base + half_lags, columns] = jnp.where(
                            from_tile, turned[tile + 1][:half_lags], turned[tile + 2][:half_lags]
                        ).astype(jnp.bfloat16)
                        hankel[slot, window, base + half_lags : base + lags, columns] = jnp.where(
                            from_tile_late, turned[tile + 1][half_lags:], turned[tile][half_lags:]
                        ).astype(jnp.bfloat16)
            rec_energy = jnp.concatenate(energies, axis=1)
            rows = slice(window * block, (window + 1) * block)
            lagged = lax.dot_general(
                sources[rows, :], hankel[slot, window], NT, preferred_element_type=jnp.float32
            )
            scale_pair = lax.rsqrt(src_energy[rows] * rec_energy + 1e-06)
            term = jnp.tanh(0.5 * math.sqrt(length) * (lagged * scale_pair))
            total = term if total is None else total + term
        return total

    def wait_rec(target, skip):
        def one(column):
            slot = target * n_col + column
            if not skip:
                rec_copy(slot, slot).wait_recv()
        for column in range(n_col):
            one(column)

    def sum_copy(other, slot):
        return pltpu.make_async_remote_copy(
            src_ref=sent.at[other], dst_ref=landed.at[slot],
            send_sem=sum_send.at[other], recv_sem=sum_recv.at[slot],
            device_id={"row": other}, device_id_type=MESH,
        )

    def send_sum(step):
        target = step + jnp.where(step >= row, 1, 0)
        wait_rec(target, False)
        sent[target] = terms_for(target, step % 2).astype(jnp.bfloat16)
        sum_copy(target, row).start()

    steps(n_row - 1, send_sum)

    for step in range(n_col - 1):
        slot = row * n_col + lax.rem(col + step + 1, n_col)
        rec_copy(slot, slot).wait_recv()
    fetch_stacks.wait()
    out_ref[...] = stacks_ref[...] + terms_for(row, (n_row - 1) % 2)

    def add_sum(step):
        other = step + jnp.where(step >= row, 1, 0)
        sum_copy(other, other).wait_recv()
        out_ref[...] += landed[other].astype(jnp.float32)

    steps(n_row - 1, add_sum)

    def sum_sent(step):
        sum_copy(lax.rem(row + step + 1, n_row), row).wait_send()

    def rec_sent(step):
        rec_copy(lax.rem(here + step + 1, n_row * n_col), here).wait_send()

    steps(n_row - 1, sum_sent)
    steps(n_row * n_col - 1, rec_sent)


def shards(n_row, n_col, src_raw, block_owner, chan_order, rec_raw, fir_taps, stacks):
    windows, per_device, length = rec_raw.shape
    block, columns = stacks.shape
    taps = fir_taps.shape[0]
    lags = columns // (n_col * per_device)
    devices = n_row * n_col
    tiles = length // LANES
    rec_rows = windows * per_device * tiles
    block_owner = block_owner.T
    rec_raw = jnp.transpose(rec_raw, (1, 0, 2))
    hbm = pl.BlockSpec(memory_space=pltpu.HBM)
    return pl.pallas_call(
        functools.partial(kernel, n_row, n_col, (taps - 1) // 2, lags),
        out_shape=jax.ShapeDtypeStruct(stacks.shape, stacks.dtype),
        in_specs=[hbm] * 6,
        out_specs=pl.BlockSpec(memory_space=pltpu.VMEM),
        scratch_shapes=[
            pltpu.VMEM(block_owner.shape, block_owner.dtype),
            pltpu.VMEM(chan_order.shape, chan_order.dtype),
            pltpu.VMEM((taps,), fir_taps.dtype),
            pltpu.VMEM(rec_raw.shape, rec_raw.dtype),
            pltpu.VMEM(src_raw.shape, src_raw.dtype),
            pltpu.VMEM(stacks.shape, stacks.dtype),
            pltpu.VMEM((1, 3 * LANES), jnp.float32),
            pltpu.VMEM((windows * block, length + 2 * LANES), jnp.bfloat16),
            pltpu.VMEM((windows * block, length), jnp.bfloat16),
            pltpu.VMEM((-(-windows * per_device // 16) * 16, length + 2 * LANES), jnp.float32),
            pltpu.VMEM((rec_rows, LANES), jnp.float32),
            pltpu.VMEM((devices, rec_rows, LANES), jnp.bfloat16),
            pltpu.VMEM((2, windows, columns, length), jnp.bfloat16),
            pltpu.VMEM((n_row, block, columns), jnp.bfloat16),
            pltpu.VMEM((n_row, block, columns), jnp.bfloat16),
            pltpu.SemaphoreType.DMA((devices,)),
            pltpu.SemaphoreType.DMA((devices,)),
            pltpu.SemaphoreType.DMA((n_row,)),
            pltpu.SemaphoreType.DMA((n_row,)),
            pltpu.SemaphoreType.DMA((6,)),
        ],
        compiler_params=pltpu.CompilerParams(
            collective_id=0, has_side_effects=True, vmem_limit_bytes=32 * 1024 * 1024
        ),
        cost_estimate=pl.CostEstimate(
            flops=2 * windows * block * length * columns * n_row,
            transcendentals=2 * windows * block * columns * n_row,
            bytes_accessed=2 * windows * block * length + 8 * block * columns,
        ),
    )(*(
        pltpu.with_memory_space_constraint(operand, pltpu.HBM)
        for operand in (block_owner, chan_order, fir_taps, rec_raw, src_raw, stacks)
    ))


def solution(mesh):
    in_specs = (
        P(("grp", "row"), None, "col", None),
        P("grp", "col"),
        P("grp", "col", None),
        P("grp", ("row", "col"), None),
        P(),
        P(("grp", "col"), "row"),
    )
    out_specs = P(("grp", "col"), "row")
    body = functools.partial(shards, mesh.shape["row"], mesh.shape["col"])
    return jax.shard_map(body, mesh=mesh, in_specs=in_specs, out_specs=out_specs, check_vma=False)
```

```python
import functools
import math

import jax
import jax.numpy as jnp
from jax import lax
from jax.experimental import pallas as pl
from jax.experimental.pallas import tpu as pltpu
from jax.sharding import PartitionSpec as P

MESH = pl.DeviceIdType.MESH
LANES = 128
OUT_TILE = 256
PARTS = 4
NT = (((1,), (1,)), ((), ()))
TN = (((0,), (0,)), ((), ()))


def steps(count, body):
    if count <= 16:
        for index in range(count):
            body(index)
    else:
        pl.loop(0, count)(body)


def kernel(
    n_row, n_col, half_taps, lags,
    owner_hbm, order_hbm, taps_hbm, rec_hbm, src_hbm, stacks_hbm,
    out_ref,
    owner_ref, order_ref, taps_ref, rec_ref, src_ref, stacks_ref, taps_row, padded, sources, rec_padded, rec_block, rec_all, hankel, sent, landed,
    rec_send, rec_recv, sum_send, sum_recv, load_sem,
):
    row, col = lax.axis_index("row"), lax.axis_index("col")
    here = row * n_col + col
    per_device, windows, length = rec_ref.shape
    block = src_ref.shape[2]
    half_lags = lags // 2
    tiles = length // LANES
    out_tiles = length // OUT_TILE
    reach = OUT_TILE + 2 * LANES

    fetched = [
        pltpu.make_async_copy(source, target, load_sem.at[index])
        for index, (source, target) in enumerate([
            (taps_hbm, taps_ref), (rec_hbm, rec_ref), (src_hbm, src_ref),
            (order_hbm, order_ref), (owner_hbm, owner_ref), (stacks_hbm, stacks_ref),
        ])
    ]
    for copy in fetched:
        copy.start()
    fetch_taps, fetch_rec, fetch_src, fetch_order, fetch_owner, fetch_stacks = fetched

    barrier = pltpu.get_barrier_semaphore()

    def greet(step):
        other = lax.rem(here + step + 1, n_row * n_col)
        pl.semaphore_signal(
            barrier, inc=1,
            device_id={"row": other // n_col, "col": lax.rem(other, n_col)},
            device_id_type=MESH,
        )

    steps(n_row * n_col - 1, greet)

    flip_row = lax.broadcasted_iota(jnp.int32, (LANES, LANES), 0)
    flip_col = lax.broadcasted_iota(jnp.int32, (LANES, LANES), 1)
    flip = jnp.where(flip_row + flip_col == LANES - 1, 1.0, 0.0).astype(jnp.bfloat16)
    empty = jnp.zeros((LANES, LANES), jnp.bfloat16)
    taps_row[...] = jnp.zeros_like(taps_row)
    rec_padded[...] = jnp.zeros_like(rec_padded)
    padded[:, :LANES] = jnp.zeros((windows * block, LANES), jnp.bfloat16)
    padded[:, LANES + length :] = jnp.zeros((windows * block, LANES), jnp.bfloat16)
    fetch_taps.wait()
    taps_row[:, : taps_ref.shape[0]] = taps_ref[...].astype(jnp.float32).reshape((1, -1))
    band = pltpu.roll(
        jnp.broadcast_to(taps_row[...], (LANES, 3 * LANES)),
        LANES - half_taps, axis=1, stride=1, stride_axis=0,
    ).astype(jnp.bfloat16)
    band = jnp.dot(flip, band, preferred_element_type=jnp.float32).astype(jnp.bfloat16)
    band = jnp.concatenate(
        [jnp.concatenate([empty, band], axis=1), jnp.concatenate([band, empty], axis=1)], axis=0
    )

    fetch_rec.wait()
    for window in range(windows):
        for index in range(per_device):
            at = window * per_device + index
            rec_padded[at : at + 1, LANES : LANES + length] = rec_ref[
                index, window : window + 1
            ].astype(jnp.float32)
    for tile in range(out_tiles):
        taken = rec_padded[:, tile * OUT_TILE : tile * OUT_TILE + reach].astype(jnp.bfloat16)
        made = lax.dot_general(taken, band, NT, preferred_element_type=jnp.float32)
        for part in range(OUT_TILE // LANES):
            place = (out_tiles - 1 - tile) * (OUT_TILE // LANES) + part
            for at in range(windows * per_device):
                rec_block[at * tiles + place : at * tiles + place + 1, :] = made[
                    at : at + 1, part * LANES : (part + 1) * LANES
                ]
    rec_all[here] = rec_block[...].astype(jnp.bfloat16)

    pl.semaphore_wait(barrier, n_row * n_col - 1)

    def rec_copy(other, slot):
        return pltpu.make_async_remote_copy(
            src_ref=rec_all.at[slot], dst_ref=rec_all.at[slot],
            send_sem=rec_send.at[other], recv_sem=rec_recv.at[slot],
            device_id={"row": other // n_col, "col": lax.rem(other, n_col)},
            device_id_type=MESH,
        )

    def send_rec(step):
        first = (n_row // 2) * n_col
        if isinstance(step, int):
            other = lax.rem(here + first + step + (step + first >= n_row * n_col), n_row * n_col)
        else:
            other = lax.rem(
                here + jnp.where(step + first >= n_row * n_col, step + first + 1, step + first),
                n_row * n_col,
            )
        rec_copy(other, here).start()

    steps(n_row * n_col - 1, send_rec)

    fetch_src.wait()
    fetch_order.wait()
    fetch_owner.wait()
    for window in range(windows):
        position = lax.broadcasted_iota(jnp.int32, (block, block), 0)
        wanted = jnp.where(
            jnp.broadcast_to(owner_ref[:, window : window + 1], (1, block)) == row,
            order_ref[window], -1,
        )
        chosen = jnp.where(position == wanted, 1.0, 0.0).astype(jnp.bfloat16)
        padded[window * block : (window + 1) * block, LANES : LANES + length] = lax.dot_general(
            chosen, src_ref[0, window], TN, preferred_element_type=jnp.float32
        ).astype(jnp.bfloat16)
    src_energy = jnp.zeros((windows * block, 1), jnp.float32)
    for tile in range(out_tiles):
        made = lax.dot_general(
            padded[:, tile * OUT_TILE : tile * OUT_TILE + reach], band, NT,
            preferred_element_type=jnp.float32,
        ).astype(jnp.bfloat16)
        place = (out_tiles - 1 - tile) * OUT_TILE
        sources[:, place : place + OUT_TILE] = made
        src_energy += jnp.sum(jnp.square(made.astype(jnp.float32)), axis=1, keepdims=True)

    lag = lax.broadcasted_iota(jnp.int32, (half_lags, LANES), 0)
    lane = lax.broadcasted_iota(jnp.int32, (half_lags, LANES), 1)
    from_tile = lane < LANES - half_lags + lag
    from_tile_late = lane >= lag
    nothing = jnp.zeros((lags, LANES), jnp.float32)

    def terms_for(target, slot):
        total = None
        for window in range(windows):
            energies = []
            for column in range(n_col):
                for index in range(per_device):
                    first = (window * per_device + index) * tiles
                    trace = rec_all[target * n_col + column].astype(jnp.float32)[
                        first : first + tiles, :
                    ]
                    energy = jnp.sum(
                        jnp.sum(jnp.square(trace), axis=0, keepdims=True), axis=1, keepdims=True
                    )
                    energies.append(jnp.broadcast_to(energy, (1, lags)))
                    turned = [
                        pltpu.roll(
                            jnp.broadcast_to(trace[tile : tile + 1, :], (lags, LANES)),
                            LANES - half_lags, axis=1, stride=1, stride_axis=0,
                        )
                        for tile in range(tiles)
                    ]
                    turned = [nothing] + turned + [nothing]
                    base = (column * per_device + index) * lags
                    for tile in range(tiles):
                        columns = slice(tile * LANES, (tile + 1) * LANES)
                        hankel[slot, window, base : base + half_lags, columns] = jnp.where(
                            from_tile, turned[tile + 1][:half_lags], turned[tile + 2][:half_lags]
                        ).astype(jnp.bfloat16)
                        hankel[slot, window, base + half_lags : base + lags, columns] = jnp.where(
                            from_tile_late, turned[tile + 1][half_lags:], turned[tile][half_lags:]
                        ).astype(jnp.bfloat16)
            rec_energy = jnp.concatenate(energies, axis=1)
            rows = slice(window * block, (window + 1) * block)
            lagged = lax.dot_general(
                sources[rows, :], hankel[slot, window], NT, preferred_element_type=jnp.float32
            )
            scale_pair = lax.rsqrt(src_energy[rows] * rec_energy + 1e-06)
            term = jnp.tanh(0.5 * math.sqrt(length) * (lagged * scale_pair))
            total = term if total is None else total + term
        return total

    def wait_rec(target, skip):
        def one(column):
            slot = target * n_col + column
            if not skip:
                rec_copy(slot, slot).wait_recv()
        for column in range(n_col):
            one(column)

    parts = sum_send.shape[1]
    depth = block // parts

    def sum_copies(other, slot):
        return [
            pltpu.make_async_remote_copy(
                src_ref=sent.at[other, pl.ds(part * depth, depth)],
                dst_ref=landed.at[slot, pl.ds(part * depth, depth)],
                send_sem=sum_send.at[other, part], recv_sem=sum_recv.at[slot, part],
                device_id={"row": other}, device_id_type=MESH,
            )
            for part in range(parts)
        ]

    def send_sum(step):
        shift = n_row // 2 + step
        shift = shift + (shift >= n_row) if isinstance(shift, int) else jnp.where(
            shift >= n_row, shift + 1, shift
        )
        target = lax.rem(row + shift, n_row)
        wait_rec(target, False)
        sent[target] = terms_for(target, step % 2).astype(jnp.bfloat16)
        for copy in sum_copies(target, row):
            copy.start()

    steps(n_row - 1, send_sum)

    for step in range(n_col - 1):
        slot = row * n_col + lax.rem(col + step + 1, n_col)
        rec_copy(slot, slot).wait_recv()
    fetch_stacks.wait()
    out_ref[...] = stacks_ref[...] + terms_for(row, (n_row - 1) % 2)

    def add_sum(step):
        other = lax.rem(row + n_row // 2 + step + (step + n_row // 2 >= n_row), n_row)
        for copy in sum_copies(other, other):
            copy.wait_recv()
        out_ref[...] += landed[other].astype(jnp.float32)

    steps(n_row - 1, add_sum)

    def sum_sent(step):
        for copy in sum_copies(lax.rem(row + step + 1, n_row), row):
            copy.wait_send()

    def rec_sent(step):
        rec_copy(lax.rem(here + step + 1, n_row * n_col), here).wait_send()

    steps(n_row - 1, sum_sent)
    steps(n_row * n_col - 1, rec_sent)


def shards(n_row, n_col, src_raw, block_owner, chan_order, rec_raw, fir_taps, stacks):
    windows, per_device, length = rec_raw.shape
    block, columns = stacks.shape
    taps = fir_taps.shape[0]
    lags = columns // (n_col * per_device)
    devices = n_row * n_col
    tiles = length // LANES
    rec_rows = windows * per_device * tiles
    block_owner = block_owner.T
    rec_raw = jnp.transpose(rec_raw, (1, 0, 2))
    hbm = pl.BlockSpec(memory_space=pltpu.HBM)
    return pl.pallas_call(
        functools.partial(kernel, n_row, n_col, (taps - 1) // 2, lags),
        out_shape=jax.ShapeDtypeStruct(stacks.shape, stacks.dtype),
        in_specs=[hbm] * 6,
        out_specs=pl.BlockSpec(memory_space=pltpu.VMEM),
        scratch_shapes=[
            pltpu.VMEM(block_owner.shape, block_owner.dtype),
            pltpu.VMEM(chan_order.shape, chan_order.dtype),
            pltpu.VMEM((taps,), fir_taps.dtype),
            pltpu.VMEM(rec_raw.shape, rec_raw.dtype),
            pltpu.VMEM(src_raw.shape, src_raw.dtype),
            pltpu.VMEM(stacks.shape, stacks.dtype),
            pltpu.VMEM((1, 3 * LANES), jnp.float32),
            pltpu.VMEM((windows * block, length + 2 * LANES), jnp.bfloat16),
            pltpu.VMEM((windows * block, length), jnp.bfloat16),
            pltpu.VMEM((-(-windows * per_device // 16) * 16, length + 2 * LANES), jnp.float32),
            pltpu.VMEM((rec_rows, LANES), jnp.float32),
            pltpu.VMEM((devices, rec_rows, LANES), jnp.bfloat16),
            pltpu.VMEM((2, windows, columns, length), jnp.bfloat16),
            pltpu.VMEM((n_row, block, columns), jnp.bfloat16),
            pltpu.VMEM((n_row, block, columns), jnp.bfloat16),
            pltpu.SemaphoreType.DMA((devices,)),
            pltpu.SemaphoreType.DMA((devices,)),
            pltpu.SemaphoreType.DMA((n_row, PARTS)),
            pltpu.SemaphoreType.DMA((n_row, PARTS)),
            pltpu.SemaphoreType.DMA((6,)),
        ],
        compiler_params=pltpu.CompilerParams(
            collective_id=0, has_side_effects=True, vmem_limit_bytes=32 * 1024 * 1024
        ),
        cost_estimate=pl.CostEstimate(
            flops=2 * windows * block * length * columns * n_row,
            transcendentals=2 * windows * block * columns * n_row,
            bytes_accessed=2 * windows * block * length + 8 * block * columns,
        ),
    )(*(
        pltpu.with_memory_space_constraint(operand, pltpu.HBM)
        for operand in (block_owner, chan_order, fir_taps, rec_raw, src_raw, stacks)
    ))


def solution(mesh):
    in_specs = (
        P(("grp", "row"), None, "col", None),
        P("grp", "col"),
        P("grp", "col", None),
        P("grp", ("row", "col"), None),
        P(),
        P(("grp", "col"), "row"),
    )
    out_specs = P(("grp", "col"), "row")
    body = functools.partial(shards, mesh.shape["row"], mesh.shape["col"])
    return jax.shard_map(body, mesh=mesh, in_specs=in_specs, out_specs=out_specs, check_vma=False)
```

```python
import functools
import math

import jax
import jax.numpy as jnp
from jax import lax
from jax.experimental import pallas as pl
from jax.experimental.pallas import tpu as pltpu
from jax.sharding import PartitionSpec as P

MESH = pl.DeviceIdType.MESH
LANES = 128
OUT_TILE = 256
NT = (((1,), (1,)), ((), ()))
TN = (((0,), (0,)), ((), ()))


def steps(count, body):
    if count <= 16:
        for index in range(count):
            body(index)
    else:
        pl.loop(0, count)(body)


def kernel(
    n_row, n_col, half_taps, lags,
    owner_hbm, order_hbm, taps_hbm, rec_hbm, src_hbm, stacks_hbm,
    out_ref,
    owner_ref, order_ref, taps_ref, rec_ref, src_ref, stacks_ref, taps_row, padded, sources, rec_padded, rec_block, rec_all, hankel, sent, landed,
    rec_send, rec_recv, sum_send, sum_recv, load_sem,
):
    row, col = lax.axis_index("row"), lax.axis_index("col")
    here = row * n_col + col
    per_device, windows, length = rec_ref.shape
    block = src_ref.shape[2]
    half_lags = lags // 2
    tiles = length // LANES
    out_tiles = length // OUT_TILE
    reach = OUT_TILE + 2 * LANES

    fetched = [
        pltpu.make_async_copy(source, target, load_sem.at[index])
        for index, (source, target) in enumerate([
            (taps_hbm, taps_ref), (rec_hbm, rec_ref), (src_hbm, src_ref),
            (order_hbm, order_ref), (owner_hbm, owner_ref), (stacks_hbm, stacks_ref),
        ])
    ]
    for copy in fetched:
        copy.start()
    fetch_taps, fetch_rec, fetch_src, fetch_order, fetch_owner, fetch_stacks = fetched

    barrier = pltpu.get_barrier_semaphore()

    def greet(step):
        other = lax.rem(here + step + 1, n_row * n_col)
        pl.semaphore_signal(
            barrier, inc=1,
            device_id={"row": other // n_col, "col": lax.rem(other, n_col)},
            device_id_type=MESH,
        )

    steps(n_row * n_col - 1, greet)

    flip_row = lax.broadcasted_iota(jnp.int32, (LANES, LANES), 0)
    flip_col = lax.broadcasted_iota(jnp.int32, (LANES, LANES), 1)
    flip = jnp.where(flip_row + flip_col == LANES - 1, 1.0, 0.0).astype(jnp.bfloat16)
    empty = jnp.zeros((LANES, LANES), jnp.bfloat16)
    taps_row[...] = jnp.zeros_like(taps_row)
    rec_padded[...] = jnp.zeros_like(rec_padded)
    padded[:, :LANES] = jnp.zeros((windows * block, LANES), jnp.bfloat16)
    padded[:, LANES + length :] = jnp.zeros((windows * block, LANES), jnp.bfloat16)
    fetch_taps.wait()
    taps_row[:, : taps_ref.shape[0]] = taps_ref[...].astype(jnp.float32).reshape((1, -1))
    band = pltpu.roll(
        jnp.broadcast_to(taps_row[...], (LANES, 3 * LANES)),
        LANES - half_taps, axis=1, stride=1, stride_axis=0,
    ).astype(jnp.bfloat16)
    band = jnp.dot(flip, band, preferred_element_type=jnp.float32).astype(jnp.bfloat16)
    band = jnp.concatenate(
        [jnp.concatenate([empty, band], axis=1), jnp.concatenate([band, empty], axis=1)], axis=0
    )

    fetch_rec.wait()
    for window in range(windows):
        for index in range(per_device):
            at = window * per_device + index
            rec_padded[at : at + 1, LANES : LANES + length] = rec_ref[
                index, window : window + 1
            ].astype(jnp.float32)
    for tile in range(out_tiles):
        taken = rec_padded[:, tile * OUT_TILE : tile * OUT_TILE + reach].astype(jnp.bfloat16)
        made = lax.dot_general(taken, band, NT, preferred_element_type=jnp.float32)
        for part in range(OUT_TILE // LANES):
            place = (out_tiles - 1 - tile) * (OUT_TILE // LANES) + part
            for at in range(windows * per_device):
                rec_block[at * tiles + place : at * tiles + place + 1, :] = made[
                    at : at + 1, part * LANES : (part + 1) * LANES
                ]
    rec_all[here] = rec_block[...].astype(jnp.bfloat16)

    pl.semaphore_wait(barrier, n_row * n_col - 1)

    def rec_copy(other, slot):
        return pltpu.make_async_remote_copy(
            src_ref=rec_all.at[slot], dst_ref=rec_all.at[slot],
            send_sem=rec_send.at[other], recv_sem=rec_recv.at[slot],
            device_id={"row": other // n_col, "col": lax.rem(other, n_col)},
            device_id_type=MESH,
        )

    def send_rec(step):
        first = (n_row // 2) * n_col
        if isinstance(step, int):
            other = lax.rem(here + first + step + (step + first >= n_row * n_col), n_row * n_col)
        else:
            other = lax.rem(
                here + jnp.where(step + first >= n_row * n_col, step + first + 1, step + first),
                n_row * n_col,
            )
        rec_copy(other, here).start()

    steps(n_row * n_col - 1, send_rec)

    fetch_src.wait()
    fetch_order.wait()
    fetch_owner.wait()
    for window in range(windows):
        position = lax.broadcasted_iota(jnp.int32, (block, block), 0)
        wanted = jnp.where(
            jnp.broadcast_to(owner_ref[:, window : window + 1], (1, block)) == row,
            order_ref[window], -1,
        )
        chosen = jnp.where(position == wanted, 1.0, 0.0).astype(jnp.bfloat16)
        padded[window * block : (window + 1) * block, LANES : LANES + length] = lax.dot_general(
            chosen, src_ref[0, window], TN, preferred_element_type=jnp.float32
        ).astype(jnp.bfloat16)
    src_energy = jnp.zeros((windows * block, 1), jnp.float32)
    for tile in range(out_tiles):
        made = lax.dot_general(
            padded[:, tile * OUT_TILE : tile * OUT_TILE + reach], band, NT,
            preferred_element_type=jnp.float32,
        ).astype(jnp.bfloat16)
        place = (out_tiles - 1 - tile) * OUT_TILE
        sources[:, place : place + OUT_TILE] = made
        src_energy += jnp.sum(jnp.square(made.astype(jnp.float32)), axis=1, keepdims=True)

    lag = lax.broadcasted_iota(jnp.int32, (half_lags, LANES), 0)
    lane = lax.broadcasted_iota(jnp.int32, (half_lags, LANES), 1)
    from_tile = lane < LANES - half_lags + lag
    from_tile_late = lane >= lag
    nothing = jnp.zeros((lags, LANES), jnp.float32)

    def terms_for(target, slot):
        total = None
        for window in range(windows):
            energies = []
            for column in range(n_col):
                for index in range(per_device):
                    first = (window * per_device + index) * tiles
                    trace = rec_all[target * n_col + column].astype(jnp.float32)[
                        first : first + tiles, :
                    ]
                    energy = jnp.sum(
                        jnp.sum(jnp.square(trace), axis=0, keepdims=True), axis=1, keepdims=True
                    )
                    energies.append(jnp.broadcast_to(energy, (1, lags)))
                    turned = [
                        pltpu.roll(
                            jnp.broadcast_to(trace[tile : tile + 1, :], (lags, LANES)),
                            LANES - half_lags, axis=1, stride=1, stride_axis=0,
                        )
                        for tile in range(tiles)
                    ]
                    turned = [nothing] + turned + [nothing]
                    base = (column * per_device + index) * lags
                    for tile in range(tiles):
                        columns = slice(tile * LANES, (tile + 1) * LANES)
                        hankel[slot, window, base : base + half_lags, columns] = jnp.where(
                            from_tile, turned[tile + 1][:half_lags], turned[tile + 2][:half_lags]
                        ).astype(jnp.bfloat16)
                        hankel[slot, window, base + half_lags : base + lags, columns] = jnp.where(
                            from_tile_late, turned[tile + 1][half_lags:], turned[tile][half_lags:]
                        ).astype(jnp.bfloat16)
            rec_energy = jnp.concatenate(energies, axis=1)
            rows = slice(window * block, (window + 1) * block)
            lagged = lax.dot_general(
                hankel[slot, window], sources[rows, :], NT, preferred_element_type=jnp.float32
            ).T
            scale_pair = lax.rsqrt(src_energy[rows] * rec_energy + 1e-06)
            term = jnp.tanh(0.5 * math.sqrt(length) * (lagged * scale_pair))
            total = term if total is None else total + term
        return total

    def wait_rec(target, skip):
        def one(column):
            slot = target * n_col + column
            if not skip:
                rec_copy(slot, slot).wait_recv()
        for column in range(n_col):
            one(column)

    def sum_copy(other, slot):
        return pltpu.make_async_remote_copy(
            src_ref=sent.at[other], dst_ref=landed.at[slot],
            send_sem=sum_send.at[other], recv_sem=sum_recv.at[slot],
            device_id={"row": other}, device_id_type=MESH,
        )

    def send_sum(step):
        shift = n_row // 2 + step
        shift = shift + (shift >= n_row) if isinstance(shift, int) else jnp.where(
            shift >= n_row, shift + 1, shift
        )
        target = lax.rem(row + shift, n_row)
        wait_rec(target, False)
        sent[target] = terms_for(target, step % 2).astype(jnp.bfloat16)
        sum_copy(target, row).start()

    steps(n_row - 1, send_sum)

    for step in range(n_col - 1):
        slot = row * n_col + lax.rem(col + step + 1, n_col)
        rec_copy(slot, slot).wait_recv()
    fetch_stacks.wait()
    out_ref[...] = stacks_ref[...] + terms_for(row, (n_row - 1) % 2)

    def add_sum(step):
        other = lax.rem(row + n_row // 2 + step + (step + n_row // 2 >= n_row), n_row)
        sum_copy(other, other).wait_recv()
        out_ref[...] += landed[other].astype(jnp.float32)

    steps(n_row - 1, add_sum)

    def sum_sent(step):
        sum_copy(lax.rem(row + step + 1, n_row), row).wait_send()

    def rec_sent(step):
        rec_copy(lax.rem(here + step + 1, n_row * n_col), here).wait_send()

    steps(n_row - 1, sum_sent)
    steps(n_row * n_col - 1, rec_sent)


def shards(n_row, n_col, src_raw, block_owner, chan_order, rec_raw, fir_taps, stacks):
    windows, per_device, length = rec_raw.shape
    block, columns = stacks.shape
    taps = fir_taps.shape[0]
    lags = columns // (n_col * per_device)
    devices = n_row * n_col
    tiles = length // LANES
    rec_rows = windows * per_device * tiles
    block_owner = block_owner.T
    rec_raw = jnp.transpose(rec_raw, (1, 0, 2))
    hbm = pl.BlockSpec(memory_space=pltpu.HBM)
    return pl.pallas_call(
        functools.partial(kernel, n_row, n_col, (taps - 1) // 2, lags),
        out_shape=jax.ShapeDtypeStruct(stacks.shape, stacks.dtype),
        in_specs=[hbm] * 6,
        out_specs=pl.BlockSpec(memory_space=pltpu.VMEM),
        scratch_shapes=[
            pltpu.VMEM(block_owner.shape, block_owner.dtype),
            pltpu.VMEM(chan_order.shape, chan_order.dtype),
            pltpu.VMEM((taps,), fir_taps.dtype),
            pltpu.VMEM(rec_raw.shape, rec_raw.dtype),
            pltpu.VMEM(src_raw.shape, src_raw.dtype),
            pltpu.VMEM(stacks.shape, stacks.dtype),
            pltpu.VMEM((1, 3 * LANES), jnp.float32),
            pltpu.VMEM((windows * block, length + 2 * LANES), jnp.bfloat16),
            pltpu.VMEM((windows * block, length), jnp.bfloat16),
            pltpu.VMEM((-(-windows * per_device // 16) * 16, length + 2 * LANES), jnp.float32),
            pltpu.VMEM((rec_rows, LANES), jnp.float32),
            pltpu.VMEM((devices, rec_rows, LANES), jnp.bfloat16),
            pltpu.VMEM((2, windows, columns, length), jnp.bfloat16),
            pltpu.VMEM((n_row, block, columns), jnp.bfloat16),
            pltpu.VMEM((n_row, block, columns), jnp.bfloat16),
            pltpu.SemaphoreType.DMA((devices,)),
            pltpu.SemaphoreType.DMA((devices,)),
            pltpu.SemaphoreType.DMA((n_row,)),
            pltpu.SemaphoreType.DMA((n_row,)),
            pltpu.SemaphoreType.DMA((6,)),
        ],
        compiler_params=pltpu.CompilerParams(
            collective_id=0, has_side_effects=True, vmem_limit_bytes=32 * 1024 * 1024
        ),
        cost_estimate=pl.CostEstimate(
            flops=2 * windows * block * length * columns * n_row,
            transcendentals=2 * windows * block * columns * n_row,
            bytes_accessed=2 * windows * block * length + 8 * block * columns,
        ),
    )(*(
        pltpu.with_memory_space_constraint(operand, pltpu.HBM)
        for operand in (block_owner, chan_order, fir_taps, rec_raw, src_raw, stacks)
    ))


def solution(mesh):
    in_specs = (
        P(("grp", "row"), None, "col", None),
        P("grp", "col"),
        P("grp", "col", None),
        P("grp", ("row", "col"), None),
        P(),
        P(("grp", "col"), "row"),
    )
    out_specs = P(("grp", "col"), "row")
    body = functools.partial(shards, mesh.shape["row"], mesh.shape["col"])
    return jax.shard_map(body, mesh=mesh, in_specs=in_specs, out_specs=out_specs, check_vma=False)
```
